256 devices in a mesh: dp: 8 (over x, core), vocab: 32 (over z, y).
Axes of the slice: x: 4, y: 4, z: 8, core: 2. Of those that a mesh axis runs over, the one named last changes fastest.
Arguments:
- encoder_rows: bfloat16 [64, 32, 1536], P(None, 'dp', 'vocab'), may hold values from -6 to 6
- predictor_rows: bfloat16 [64, 129, 640], P('dp'), may hold values from -6 to 6
- enc_weight: bfloat16 [1536, 640], P('dp'), may hold values from -0.15625 to 0.15625
- pred_weight: bfloat16 [640, 640], P('dp'), may hold values from -0.25 to 0.25
- out_weight: bfloat16 [640, 4096], P(None, 'vocab'), may hold values from -48 to 48
- frame_lengths: int32 [64], P('dp'), may hold values from 16 to 32
- label_lengths: int32 [64], P('dp'), may hold values from 32 to 128
- label_ids: int32 [64, 128], P('dp'), may hold values from 1 to 4095
Outputs:
- losses: float32 [64], P('dp')
The draws below stay inside these ranges and needn't reach their ends.
All inputs are finite; a program needn't handle non-finite values.
Results may differ from the reference program's by a relative error of at most 0.00035.
Values may be sent and summed in bfloat16 or wider, within the bound.
A program may use at most 128 MiB of HBM per device.

```python
import jax
import jax.numpy as jnp
from jax import lax

D = 1536
P_SIZE = 640
J = 640
VOCAB = 4096
LABELS = 128
UTTS = 64
FRAMES = 32


def draw_out_weight(key, part):
    key = jax.random.fold_in(key, 3)
    unit = jnp.clip(jax.random.normal(key, (J, VOCAB), jnp.float32), -5.0, 5.0)
    return (unit * (4.0 / J ** 0.5)).astype(jnp.bfloat16)


def draw_frame_lengths(key, part):
    key = jax.random.fold_in(key, 5)
    lengths = jax.random.randint(jax.random.fold_in(key, 1), (UTTS,), FRAMES // 2, FRAMES + 1)
    chosen = jax.random.randint(jax.random.fold_in(key, 2), (), 0, UTTS)
    return jnp.where(jnp.arange(UTTS) == chosen, FRAMES, lengths).astype(jnp.int32)


def draw_label_lengths(key, part):
    key = jax.random.fold_in(key, 7)
    lengths = jax.random.randint(jax.random.fold_in(key, 1), (UTTS,), max(1, LABELS // 4), LABELS + 1)
    chosen = jax.random.randint(jax.random.fold_in(key, 2), (), 0, UTTS)
    return jnp.where(jnp.arange(UTTS) == chosen, LABELS, lengths).astype(jnp.int32)


def place_ends(drawn, key, low, high):
    extent = drawn.shape
    place = [jax.random.randint(jax.random.fold_in(key, axis), (), 0, extent[axis]) for axis in range(len(extent))]
    drawn = drawn.at[tuple(place)].set(low)
    longest = extent.index(max(extent))
    place[longest] = (place[longest] + 1) % extent[longest]
    return drawn.at[tuple(place)].set(high)


def block_scale(stream_key, extent, split, least, largest):
    loudness = 1.0
    for axis_at, parts in split:
        steps = jax.random.uniform(jax.random.fold_in(jax.random.fold_in(stream_key, 6), axis_at), (parts,), jnp.float32, least / len(split), largest / len(split))
        loudness = loudness * jnp.repeat(jnp.exp(steps), extent[axis_at] // parts).reshape((-1,) + (1,) * (len(extent) - 1 - axis_at))
    return loudness


def centred(own_key, extent, spread, most, pieces=(), kind=jnp.bfloat16):
    entries = spread * jax.random.normal(own_key, extent, jnp.float32)
    if pieces:
        entries = entries * block_scale(own_key, extent, pieces, -0.22, 0.18)
    return jnp.clip(entries, -most, most).astype(kind)


def setup_inputs(seed: int = 0) -> dict:
    keys = jax.random.split(jax.random.key(seed), 9)
    return {
        "encoder_rows": centred(keys[0], (UTTS, FRAMES, D), 1.0, 6.0, ((1, 8), (2, 32))),
        "predictor_rows": centred(keys[1], (UTTS, LABELS + 1, P_SIZE), 1.0, 6.0, ((0, 8),)),
        "enc_weight": centred(keys[2], (D, J), D ** -0.5, 0.15625, ((0, 8),)),
        "pred_weight": centred(keys[3], (P_SIZE, J), P_SIZE ** -0.5, 0.25, ((0, 8),)),
        "out_weight": draw_out_weight(jax.random.fold_in(keys[8], 71), 0),
        "frame_lengths": draw_frame_lengths(jax.random.fold_in(keys[8], 71), 0),
        "label_lengths": draw_label_lengths(jax.random.fold_in(keys[8], 71), 0),
        "label_ids": place_ends(jax.random.randint(keys[7], (UTTS, LABELS), 1, VOCAB), jax.random.fold_in(keys[7], 1), 1, VOCAB - 1).astype(jnp.int32),
    }


neg_floor = -1.0e30


def combine(earlier, later):
    return (earlier[0] + later[0], jnp.logaddexp(later[1], later[0] + earlier[1]))


def lattice(blank_lp, label_lp, frame_lengths, label_lengths):
    batch_rows, frames, positions = blank_lp.shape
    u_iota = jnp.arange(positions).astype(jnp.int32)
    start_row = jnp.where(u_iota[None, :] == 0, jnp.zeros((batch_rows, positions), jnp.float32), jnp.full((batch_rows, positions), neg_floor, jnp.float32))

    def advance(state, inputs):
        incoming, result = state
        blank_t, label_t, frame_index = inputs
        gains = jnp.concatenate([jnp.zeros((batch_rows, 1), jnp.float32), label_t[:, :-1]], axis=1)
        unused, alpha_t = lax.associative_scan(combine, (gains, incoming), axis=1)
        ending = alpha_t + blank_t
        here = jnp.sum(jnp.where(u_iota[None, :] == label_lengths[:, None], ending, jnp.zeros_like(ending)), axis=1)
        result = jnp.where(frame_index == frame_lengths - 1, here, result)
        return (ending, result), None

    inputs = (jnp.moveaxis(blank_lp, 1, 0), jnp.moveaxis(label_lp, 1, 0), jnp.arange(frames).astype(jnp.int32))
    (unused, result), unused_out = lax.scan(advance, (start_row, jnp.zeros((batch_rows,), jnp.float32)), inputs)
    return -result / (frame_lengths + label_lengths).astype(jnp.float32)


def reference(encoder_rows, predictor_rows, enc_weight, pred_weight, out_weight, frame_lengths, label_lengths, label_ids):
    utterances, frames, feature_width = encoder_rows.shape
    positions = predictor_rows.shape[1]
    joint_width = enc_weight.shape[1]
    enc_proj = jnp.dot(encoder_rows.reshape(-1, feature_width), enc_weight, preferred_element_type=jnp.float32).astype(jnp.bfloat16).reshape(utterances, frames, joint_width)
    pred_proj = jnp.dot(predictor_rows.reshape(-1, predictor_rows.shape[2]), pred_weight, preferred_element_type=jnp.float32).astype(jnp.bfloat16).reshape(utterances, positions, joint_width)
    padded_labels = jnp.concatenate([label_ids, jnp.zeros((utterances, 1), jnp.int32)], axis=1)

    def one_utterance(inputs):
        enc_rows, pred_rows, label_row = inputs
        row_ids = jnp.broadcast_to(label_row[None, :], (8, positions)).reshape(-1)

        def one_block(offset):
            enc_block = lax.dynamic_slice_in_dim(enc_rows, offset, 8, 0)
            hidden = jnp.tanh(enc_block.astype(jnp.float32)[:, None, :] + pred_rows.astype(jnp.float32)[None, :, :]).astype(jnp.bfloat16).reshape(-1, joint_width)
            logits = jnp.dot(hidden, out_weight, preferred_element_type=jnp.float32)
            maxima = jnp.max(logits, axis=1)
            totals = jnp.sum(jnp.exp(logits - maxima[:, None]), axis=1)
            log_norm = maxima + jnp.log(totals)
            label_val = jnp.take_along_axis(logits, row_ids[:, None], axis=1)[:, 0]
            return (logits[:, 0] - log_norm).reshape(8, positions), (label_val - log_norm).reshape(8, positions)

        blank_part, label_part = lax.map(one_block, jnp.arange(0, frames, 8).astype(jnp.int32))
        return blank_part.reshape(frames, positions), label_part.reshape(frames, positions)

    blank_lp, label_lp = lax.map(one_utterance, (enc_proj, pred_proj, padded_labels))
    return lattice(blank_lp, label_lp, frame_lengths, label_lengths)
```

```python
import functools

import jax
import jax.numpy as jnp
from jax import lax
from jax.experimental import pallas as pl
from jax.experimental.pallas import tpu as pltpu
from jax.sharding import PartitionSpec as P

MESH = pl.DeviceIdType.MESH
NY = 4
NEG = -1e30
NT = (((1,), (1,)), ((), ()))


def joint_kernel(
    ndp,
    nv,
    xin,
    prows,
    wenc,
    wpred,
    wout,
    flen,
    llen,
    labels,
    out,
    bufb,
    xp,
    bufx,
    we,
    wp,
    prow,
    part,
    enc,
    pred,
    wt,
    wlab,
    hid,
    stat,
    lp,
    lossbuf,
    state0,
    prow_sem,
    xd_s,
    xd_r,
    xz_s,
    xz_r,
    we_s,
    we_r,
    wp_s,
    wp_r,
    ring_s,
    ring_r,
    sib_s,
    sib_r,
    y_s,
    y_r,
    st_s,
    st_r,
    lo_s,
    lo_r,
):
    nz = nv // NY
    nx = ndp // 2
    i = lax.axis_index("dp")
    v = lax.axis_index("vocab")
    z = v // NY
    y = v % NY
    x = i // 2
    c = i % 2
    sib = 2 * x + (1 - c)
    frames = part.shape[1]
    width = part.shape[2]
    feat = xin.shape[2]
    quarter = frames // ndp

    def vz(s):
        return ((z + s + nz) % nz) * NY + y

    def vy(s):
        return z * NY + (y + s) % NY

    barrier = pltpu.get_barrier_semaphore()
    for s in range(1, ndp):
        pl.semaphore_signal(barrier, inc=1, device_id=((i + s) % ndp, v), device_id_type=MESH)
    for s in range(1, nz):
        pl.semaphore_signal(barrier, inc=1, device_id=(i, vz(s)), device_id_type=MESH)
    for s in range(1, NY):
        pl.semaphore_signal(barrier, inc=1, device_id=(i, vy(s)), device_id_type=MESH)

    prow_copy = pltpu.make_async_copy(prows.at[z], prow, prow_sem)
    prow_copy.start()

    bufb[i] = xin[i]
    own_wt = wout[...].astype(jnp.float32).T.astype(jnp.bfloat16)
    wt[z] = own_wt
    erow = pl.multiple_of(48 * y, 16)
    we[i] = wenc[pl.ds(erow, feat), :]
    wp[i] = wpred[...]
    stat[y, 2] = jnp.zeros(stat.shape[2:], jnp.float32)

    pl.semaphore_wait(barrier, (ndp - 1) + (nz - 1) + (NY - 1))

    def remote(src, dst, ssem, rsem, dev):
        return pltpu.make_async_remote_copy(
            src_ref=src, dst_ref=dst, send_sem=ssem, recv_sem=rsem, device_id=dev, device_id_type=MESH
        )

    sends = []

    def go(cp):
        cp.start()
        sends.append(cp)
        return cp

    xd = []
    for s in range(1, ndp):
        k = (i + s) % ndp
        xd.append(go(remote(xin.at[k], bufb.at[i], xd_s.at[s - 1], xd_r.at[s - 1], (k, v))))

    half = wt.shape[1] // 2
    my_half = pl.ds(pl.multiple_of(c * half, half), half)

    def ring_copy(origin, s, direction):
        idx = s - 1 if direction > 0 else nz // 2 + s - 1
        blk = wt.at[origin, my_half]
        return remote(blk, blk, ring_s.at[idx], ring_r.at[idx], (i, vz(direction)))

    def sib_copy(origin, idx):
        blk = wt.at[origin, my_half]
        return remote(blk, blk, sib_s.at[idx], sib_r.at[idx], (sib, v))

    n_right, n_left = nz // 2, nz - 1 - nz // 2
    rights = [go(ring_copy(z, 1, 1))]
    lefts = [go(ring_copy(z, 1, -1))]
    sibs = []

    we_c, wp_c = [], []
    for s in range(1, nx):
        dev = (2 * ((x + s) % nx) + c, v)
        we_c.append(go(remote(we.at[i], we.at[i], we_s.at[s - 1], we_r.at[s - 1], dev)))
    we_sib = [go(remote(we.at[i], we.at[i], we_s.at[nx - 1], we_r.at[nx - 1], (sib, v)))]
    for s in range(1, nx):
        dev = (2 * ((x + s) % nx) + c, v)
        wp_c.append(go(remote(wp.at[i], wp.at[i], wp_s.at[s - 1], wp_r.at[s - 1], dev)))
    wp_sib = [go(remote(wp.at[i], wp.at[i], wp_s.at[nx - 1], wp_r.at[nx - 1], (sib, v)))]

    rows = bufb.shape[0] * bufb.shape[1]
    r_io = lax.broadcasted_iota(jnp.int32, (rows, rows), 0)
    c_io = lax.broadcasted_iota(jnp.int32, (rows, rows), 1)
    src = ((r_io >> 2) & 7) * 32 + (r_io >> 5) * 4 + (r_io & 3)
    perm = jnp.where(src == c_io, 1.0, 0.0).astype(jnp.bfloat16)
    for cp in xd:
        cp.wait_recv()
    moved = jnp.dot(perm, bufb[...].reshape(rows, feat), preferred_element_type=jnp.float32)
    xp[...] = moved.astype(jnp.bfloat16).reshape(xp.shape)
    xz = []
    for s in range(1, nz):
        zt = (z + s) % nz
        xz.append(go(remote(xp.at[zt], bufx.at[z], xz_s.at[s - 1], xz_r.at[s - 1], (i, vz(s)))))
    bufx[z] = xp[z]

    def ring_step(s):
        if s <= n_right:
            rights[s - 1].wait_recv()
            origin = (z - s + nz) % nz
            if s < n_right:
                rights.append(go(ring_copy(origin, s + 1, 1)))
            sibs.append(go(sib_copy(origin, s - 1)))
        if s <= n_left:
            lefts[s - 1].wait_recv()
            origin = (z + s) % nz
            if s < n_left:
                lefts.append(go(ring_copy(origin, s + 1, -1)))
            sibs.append(go(sib_copy(origin, n_right + s - 1)))

    ring_step(1)
    for s in range(1, nx):
        we_c[s - 1].wait_recv()
        o = 2 * ((x - s + nx) % nx) + c
        we_sib.append(
            go(remote(we.at[o], we.at[o], we_s.at[nx - 1 + s], we_r.at[nx - 1 + s], (sib, v)))
        )
    ring_step(2)
    for cp in xz:
        cp.wait_recv()
    for cp in we_sib:
        cp.wait_recv()
    acc = jnp.dot(bufx[0], we[0], preferred_element_type=jnp.float32)
    for k in range(1, nz):
        acc = acc + jnp.dot(bufx[k], we[k], preferred_element_type=jnp.float32)
    part[y] = acc
    ys = []
    for s in range(1, NY):
        ys.append(go(remote(part.at[y], part.at[y], y_s.at[s - 1], y_r.at[s - 1], (i, vy(s)))))
    for s in range(1, nx):
        wp_c[s - 1].wait_recv()
        o = 2 * ((x - s + nx) % nx) + c
        wp_sib.append(
            go(remote(wp.at[o], wp.at[o], wp_s.at[nx - 1 + s], wp_r.at[nx - 1 + s], (sib, v)))
        )
    for s in range(3, max(n_right, n_left) + 1):
        ring_step(s)
    for cp in wp_sib:
        cp.wait_recv()
    prow_copy.wait()
    positions = prow.shape[0]
    pp = jnp.dot(prow[...], wp[...].reshape(-1, width), preferred_element_type=jnp.float32)
    pred[...] = jnp.zeros_like(pred)
    pred[0:positions, :] = pp.astype(jnp.bfloat16).astype(jnp.float32)
    for cp in ys:
        cp.wait_recv()
    total = part[0]
    for k in range(1, NY):
        total = total + part[k]
    enc[...] = total.astype(jnp.bfloat16).astype(jnp.float32)
    for cp in sibs:
        cp.wait_recv()

    nvoc = wt.shape[0] * wt.shape[1]
    block_cols = wt.shape[1]
    upad = wlab.shape[0] * 8
    n_lab = labels.shape[1]
    lab_rows = jnp.broadcast_to(labels[pl.ds(z, 1), :], (n_lab, n_lab)).astype(jnp.float32).T
    lab_rows = jnp.concatenate([lab_rows, jnp.zeros((upad - n_lab, n_lab), jnp.float32)], axis=0)
    lane = lax.broadcasted_iota(jnp.int32, (upad, n_lab), 1)
    lab_acc = jnp.zeros((upad, width), jnp.float32)
    for k in range(wt.shape[0]):
        gid = (lane + (k * NY + y) * block_cols).astype(jnp.float32)
        onehot = jnp.where(lab_rows == gid, 1.0, 0.0).astype(jnp.bfloat16)
        lab_acc = lab_acc + jnp.dot(onehot, wt[k], preferred_element_type=jnp.float32)
    wlab[...] = jnp.zeros_like(wlab)
    for k in range(wlab.shape[0]):
        wlab[k, 0:8, :] = lab_acc[8 * k : 8 * k + 8, :].astype(jnp.bfloat16)

    cells = 8 * frames
    sub_r = lax.broadcasted_iota(jnp.int32, (16, cells), 0)
    sub_l = lax.broadcasted_iota(jnp.int32, (16, cells), 1) // frames
    label_mask = sub_r == sub_l
    chunk = 2

    def block(g, k):
        kk = g * 8 + k
        ev = enc[...]
        for s in range(8):
            h = jnp.tanh(ev + pred[pl.ds(kk * 8 + s, 1), :])
            hid[s * frames : (s + 1) * frames, :] = h.astype(jnp.bfloat16)
        hv = hid[...]
        ms, ss = [], []
        blank = None
        for q in range(wt.shape[0] // chunk):
            w = wt[q * chunk : (q + 1) * chunk].reshape(chunk * block_cols, width)
            lg = lax.dot_general(w, hv, NT, preferred_element_type=jnp.float32)
            if q == 0:
                blank = lg[0:1, :]
            m = jnp.max(lg, axis=0, keepdims=True)
            ms.append(m)
            ss.append(jnp.sum(jnp.exp(lg - m), axis=0, keepdims=True))
        ll = lax.dot_general(wlab[kk], hv, NT, preferred_element_type=jnp.float32)
        lab = jnp.sum(jnp.where(label_mask, ll, 0.0), axis=0, keepdims=True)
        top = functools.reduce(jnp.maximum, ms)
        tot = functools.reduce(jnp.add, [a * jnp.exp(b - top) for a, b in zip(ss, ms)])
        stat[y, g, 0, pl.ds(k, 1), :] = top + jnp.log(tot)
        stat[y, g, 1, pl.ds(k, 1), :] = lab
        stat[y, g, 2, pl.ds(k, 1), :] = blank

    n_blocks = wlab.shape[0]
    sts = []
    for g in range(stat.shape[1]):
        lax.fori_loop(0, min(8, n_blocks - 8 * g), lambda k, u, g=g: (block(g, k), u)[1], 0)
        for s in range(1, NY):
            idx = g * (NY - 1) + s - 1
            sts.append(
                go(remote(stat.at[y, g], stat.at[y, g], st_s.at[idx], st_r.at[idx], (i, vy(s))))
            )
    for cp in sts:
        cp.wait_recv()

    for g in range(stat.shape[1]):
        lses = [stat[k, g, 0] for k in range(NY)]
        top = functools.reduce(jnp.maximum, lses)
        log_norm = top + jnp.log(functools.reduce(jnp.add, [jnp.exp(a - top) for a in lses]))
        label_lp = functools.reduce(jnp.add, [stat[k, g, 1] for k in range(NY)]) - log_norm
        blank_lp = stat[0, g, 2] - log_norm
        for a, val in enumerate((blank_lp, label_lp)):
            for s in range(8):
                h = val[:, 128 * (s // 4) : 128 * (s // 4) + 128]
                if s % 4:
                    h = pltpu.roll(h, 128 - 32 * (s % 4), 1)
                lp[a, pl.ds(64 * g + s, 8, stride=8), :] = h
    lanes = lax.broadcasted_iota(jnp.int32, lp.shape[1:], 1)
    for a in range(2):
        val = lp[a]
        for bit in range(5):
            val = jnp.where((lanes >> bit) & 1 == 1, pltpu.roll(val, 1 << bit, 0), val)
        lp[a] = val

    t_len = flen[z]
    u_len = llen[z]
    lane8 = lax.broadcasted_iota(jnp.int32, (8, 128), 1)
    first = lane8 == 0
    when = jnp.where(lane8 == t_len - 1, t_len - 1 + u_len, -1)

    def advance(d, state):
        e, m, res, resm = state
        b_d = jnp.broadcast_to(lp[0, pl.ds(d, 1), :], (8, 128))
        l_d = jnp.broadcast_to(lp[1, pl.ds(d, 1), :], (8, 128))
        ending = e + b_d
        hit = when == d
        res = jnp.where(hit, ending, res)
        resm = jnp.where(hit, m, resm)
        a = jnp.where(first, NEG, pltpu.roll(ending, 1, 1))
        cc = e + l_d
        e2 = jnp.maximum(a, cc)
        m2 = jnp.where(first, 0.0, pltpu.roll(m, 1, 1)) * jnp.exp(a - e2) + m * jnp.exp(cc - e2)
        return e2, m2, res, resm

    state0[0] = jnp.where(first, 0.0, NEG)
    state0[1] = jnp.where(first, 1.0, 0.0)
    state0[2] = jnp.zeros((8, 128), jnp.float32)
    state0[3] = jnp.ones((8, 128), jnp.float32)
    start = tuple(state0[k] for k in range(4))
    unused_e, unused_m, res, resm = lax.fori_loop(0, 160, advance, start, unroll=8)
    val = jnp.sum(res + jnp.log(resm), axis=1, keepdims=True)
    loss = -val / (t_len + u_len).astype(jnp.float32)
    lossbuf[z] = jnp.broadcast_to(loss, (8, 128))
    los = []
    for s in range(1, nz):
        los.append(
            go(remote(lossbuf.at[z], lossbuf.at[z], lo_s.at[s - 1], lo_r.at[s - 1], (i, vz(s))))
        )
    for cp in los:
        cp.wait_recv()
    for k in range(nz):
        out[k : k + 1, :] = lossbuf[k, 0:1, :]
    for cp in sends:
        cp.wait_send()


def shards(ndp, nv, encoder_rows, predictor_rows, enc_weight, pred_weight, out_weight, flen, llen, labels):
    utts, fr, feat = encoder_rows.shape
    nz = nv // NY
    per = predictor_rows.shape[0]
    positions = predictor_rows.shape[1]
    width = enc_weight.shape[1]
    frames = fr * ndp
    cols = out_weight.shape[1]
    n_blocks = (positions + 7) // 8
    groups = (n_blocks + 7) // 8
    xin = encoder_rows.reshape(ndp, per * fr, feat)
    vm = pl.BlockSpec(memory_space=pltpu.VMEM)
    sm = pl.BlockSpec(memory_space=pltpu.SMEM)
    dma = pltpu.SemaphoreType.DMA
    bf, f32 = jnp.bfloat16, jnp.float32
    nx = ndp // 2
    res = pl.pallas_call(
        functools.partial(joint_kernel, ndp, nv),
        out_shape=jax.ShapeDtypeStruct((per, 128), f32),
        in_specs=[vm, pl.BlockSpec(memory_space=pl.ANY), vm, vm, vm, sm, sm, vm],
        out_specs=vm,
        scratch_shapes=[
            pltpu.VMEM((ndp, per * fr, feat), bf),
            pltpu.VMEM((nz, frames, feat), bf),
            pltpu.VMEM((nz, frames, feat), bf),
            pltpu.VMEM((ndp, feat, width), bf),
            pltpu.VMEM((ndp, pred_weight.shape[0], width), bf),
            pltpu.VMEM((positions, predictor_rows.shape[2]), bf),
            pltpu.VMEM((NY, frames, width), f32),
            pltpu.VMEM((frames, width), f32),
            pltpu.VMEM((8 * n_blocks, width), f32),
            pltpu.VMEM((nz, cols, width), bf),
            pltpu.VMEM((n_blocks, 16, width), bf),
            pltpu.VMEM((8 * frames, width), bf),
            pltpu.VMEM((NY, groups, 3, 8, 8 * frames), f32),
            pltpu.VMEM((2, 64 * groups, 128), f32),
            pltpu.VMEM((nz, 8, 128), f32),
            pltpu.VMEM((4, 8, 128), f32),
            dma,
            dma((ndp - 1,)),
            dma((ndp - 1,)),
            dma((nz - 1,)),
            dma((nz - 1,)),
            dma((2 * nx - 1,)),
            dma((2 * nx - 1,)),
            dma((2 * nx - 1,)),
            dma((2 * nx - 1,)),
            dma((nz - 1,)),
            dma((nz - 1,)),
            dma((nz - 1,)),
            dma((nz - 1,)),
            dma((NY - 1,)),
            dma((NY - 1,)),
            dma((groups * (NY - 1),)),
            dma((groups * (NY - 1),)),
            dma((nz - 1,)),
            dma((nz - 1,)),
        ],
        compiler_params=pltpu.CompilerParams(
            collective_id=0, has_side_effects=True, vmem_limit_bytes=32 * 1024 * 1024
        ),
    )(xin, predictor_rows, enc_weight, pred_weight, out_weight, flen, llen, labels)
    return res[:, 0]


def solution(mesh):
    return jax.shard_map(
        functools.partial(shards, mesh.shape["dp"], mesh.shape["vocab"]),
        mesh=mesh,
        in_specs=(
            P(None, "dp", "vocab"),
            P("dp", None, None),
            P("dp", None),
            P("dp", None),
            P(None, "vocab"),
            P("dp"),
            P("dp"),
            P("dp", None),
        ),
        out_specs=P("dp"),
        check_vma=False,
    )
```

```python
import functools

import jax
import jax.numpy as jnp
from jax import lax
from jax.experimental import pallas as pl
from jax.experimental.pallas import tpu as pltpu
from jax.sharding import PartitionSpec as P

MESH = pl.DeviceIdType.MESH
NY = 4
NEG = -1e30
CHUNK = 256
NT = (((1,), (1,)), ((), ()))


RELS = (0, 1, -1, 2, -2, 3, -3, 4)


def lse(terms):
    if len(terms) == 1:
        return terms[0]
    top = functools.reduce(jnp.maximum, terms)
    return top + jnp.log(tree(jnp.add, [jnp.exp(a - top) for a in terms]))


def tree(op, vals):
    vals = list(vals)
    while len(vals) > 1:
        vals = [op(vals[k], vals[k + 1]) if k + 1 < len(vals) else vals[k] for k in range(0, len(vals), 2)]
    return vals[0]


def compose(lo, hi):
    n = len(lo)
    moved = [[pltpu.roll(b, a, 1) if a else b for b in lo] for a in range(n)]
    return [
        lse([hi[a] + moved[a][j - a] for a in range(n) if 0 <= j - a < n]) for j in range(2 * n - 1)
    ]


def joint_kernel(
    ndp,
    nv,
    xt_h,
    prows_h,
    wenc_h,
    wpred_h,
    wout_h,
    flen_h,
    llen_h,
    labels_h,
    out,
    xt,
    prows,
    wout,
    labels,
    flen,
    llen,
    xin,
    bufb,
    xp,
    bufx,
    we,
    wp,
    part,
    enc,
    pred,
    wt,
    wlab,
    hid_a,
    hid_b,
    last_a,
    last_b,
    lg_a,
    lg_b,
    stat,
    lp,
    band2,
    band4,
    band8,
    lossbuf,
    state0,
    in_s,
    xd_s,
    xd_r,
    xz_s,
    xz_r,
    we_s,
    we_r,
    wp_s,
    wp_r,
    ring_s,
    ring_r,
    sib_s,
    sib_r,
    y_s,
    y_r,
    st_s,
    st_r,
    lo_s,
    lo_r,
):
    nz = nv // NY
    nx = ndp // 2
    i = lax.axis_index("dp")
    v = lax.axis_index("vocab")
    z = v // NY
    y = v % NY
    x = i // 2
    c = i % 2
    sib = 2 * x + (1 - c)
    frames = part.shape[1]
    width = part.shape[2]
    feat = we.shape[1]

    def vz(s):
        return ((z + s + nz) % nz) * NY + y

    def vy(s):
        return z * NY + (y + s) % NY

    barrier = pltpu.get_barrier_semaphore()
    for s in range(1, nz):
        pl.semaphore_signal(barrier, inc=1, device_id=(i, vz(s)), device_id_type=MESH)
    for s in range(1, ndp):
        pl.semaphore_signal(barrier, inc=1, device_id=((i + s) % ndp, v), device_id_type=MESH)
    for s in range(1, NY):
        pl.semaphore_signal(barrier, inc=1, device_id=(i, vy(s)), device_id_type=MESH)

    erow = pl.multiple_of(feat * y, 16)
    loads = []
    for k, (src, dst) in enumerate(
        (
            (xt_h, xt),
            (wout_h, wout),
            (wenc_h.at[pl.ds(erow, feat)], we.at[i]),
            (wpred_h, wp.at[i]),
            (prows_h, prows),
            (labels_h, labels),
            (flen_h, flen),
            (llen_h, llen),
        )
    ):
        cp = pltpu.make_async_copy(src, dst, in_s.at[k])
        cp.start()
        loads.append(cp)

    def remote(src, dst, ssem, rsem, dev):
        return pltpu.make_async_remote_copy(
            src_ref=src, dst_ref=dst, send_sem=ssem, recv_sem=rsem, device_id=dev, device_id_type=MESH
        )

    sends = []

    def go(cp):
        cp.start()
        sends.append(cp)
        return cp

    utts = xt.shape[1]
    fr = xt.shape[0] // feat
    mine = utts * fr
    r_io = lax.broadcasted_iota(jnp.int32, (mine, utts), 0)
    u_io = lax.broadcasted_iota(jnp.int32, (mine, utts), 1)
    loads[0].wait()
    moved = None
    for f in range(fr):
        pick = jnp.where(r_io == u_io * fr + f, 1.0, 0.0).astype(jnp.bfloat16)
        one = lax.dot_general(
            pick, xt[f * feat : (f + 1) * feat, :], NT, preferred_element_type=jnp.float32
        )
        moved = one if moved is None else moved + one
    xin[...] = moved.astype(jnp.bfloat16).reshape(xin.shape)
    bufb[i] = xin[i]
    block_cols = wout.shape[1]
    loads[1].wait()
    wt[0:block_cols, :] = wout[...].astype(jnp.float32).T.astype(jnp.bfloat16)
    stat[y, 2] = jnp.zeros(stat.shape[2:], jnp.float32)
    loads[2].wait()
    loads[3].wait()

    pl.semaphore_wait(barrier, (ndp - 1) + (nz - 1) + (NY - 1))

    xd = []
    for s in range(1, ndp):
        k = (i + s) % ndp
        xd.append(go(remote(xin.at[k], bufb.at[i], xd_s.at[s - 1], xd_r.at[s - 1], (k, v))))

    half = block_cols // 2

    def ring_slot(rel):
        pos = RELS.index(rel)
        return wt.at[pl.ds(pl.multiple_of(pos * block_cols + c * half, half), half)]

    n_right, n_left = nz // 2, nz - 1 - nz // 2

    def ring_copy(s, direction):
        def rel(k):
            if direction < 0:
                return k
            return nz // 2 if 2 * k == nz else -k

        idx = s - 1 if direction > 0 else n_right + s - 1
        return remote(
            ring_slot(rel(s - 1)), ring_slot(rel(s)), ring_s.at[idx], ring_r.at[idx], (i, vz(direction))
        )

    def sib_copy(rel, idx):
        blk = ring_slot(rel)
        return remote(blk, blk, sib_s.at[idx], sib_r.at[idx], (sib, v))

    rights = [go(ring_copy(1, 1))]
    lefts = [go(ring_copy(1, -1))]
    sibs = {}

    we_c, wp_c = [], []
    for s in range(1, nx):
        dev = (2 * ((x + s) % nx) + c, v)
        we_c.append(go(remote(we.at[i], we.at[i], we_s.at[s - 1], we_r.at[s - 1], dev)))
    we_sib = [go(remote(we.at[i], we.at[i], we_s.at[nx - 1], we_r.at[nx - 1], (sib, v)))]
    for s in range(1, nx):
        dev = (2 * ((x + s) % nx) + c, v)
        wp_c.append(go(remote(wp.at[i], wp.at[i], wp_s.at[s - 1], wp_r.at[s - 1], dev)))
    wp_sib = [go(remote(wp.at[i], wp.at[i], wp_s.at[nx - 1], wp_r.at[nx - 1], (sib, v)))]

    def ring_step(s):
        if s <= n_right:
            rights[s - 1].wait_recv()
            if s < n_right:
                rights.append(go(ring_copy(s + 1, 1)))
            rel = nz // 2 if 2 * s == nz else -s
            sibs[rel] = go(sib_copy(rel, s - 1))
        if s <= n_left:
            lefts[s - 1].wait_recv()
            if s < n_left:
                lefts.append(go(ring_copy(s + 1, -1)))
            sibs[s] = go(sib_copy(s, n_right + s - 1))

    rows = bufb.shape[0] * bufb.shape[1]
    r_io = lax.broadcasted_iota(jnp.int32, (rows, rows), 0)
    c_io = lax.broadcasted_iota(jnp.int32, (rows, rows), 1)
    src = ((r_io >> 2) & 7) * 32 + (r_io >> 5) * 4 + (r_io & 3)
    perm = jnp.where(src == c_io, 1.0, 0.0).astype(jnp.bfloat16)
    ring_step(1)
    for cp in xd:
        cp.wait_recv()
    moved = jnp.dot(perm, bufb[...].reshape(rows, feat), preferred_element_type=jnp.float32)
    xp[...] = moved.astype(jnp.bfloat16).reshape(xp.shape)
    xz = []
    for s in (4, 3, 5, 2, 6, 1, 7):
        zt = (z + s) % nz
        xz.append(go(remote(xp.at[zt], bufx.at[z], xz_s.at[s - 1], xz_r.at[s - 1], (i, vz(s)))))
    bufx[z] = xp[z]

    positions = prows.shape[0] // xin.shape[0]
    upad = pred.shape[0]
    loads[4].wait()
    p_r = lax.broadcasted_iota(jnp.int32, (upad, prows.shape[0]), 0)
    p_c = lax.broadcasted_iota(jnp.int32, (upad, prows.shape[0]), 1)
    pick = jnp.where(p_c == p_r * xin.shape[0] + z, 1.0, 0.0).astype(jnp.bfloat16)
    prow = jnp.dot(pick, prows[...], preferred_element_type=jnp.float32).astype(jnp.bfloat16)

    for s in range(1, nx):
        we_c[s - 1].wait_recv()
        o = 2 * ((x - s + nx) % nx) + c
        we_sib.append(
            go(remote(we.at[o], we.at[o], we_s.at[nx - 1 + s], we_r.at[nx - 1 + s], (sib, v)))
        )
    ring_step(2)
    for cp in xz:
        cp.wait_recv()
    for cp in we_sib:
        cp.wait_recv()
    part[y] = tree(
        jnp.add, [jnp.dot(bufx[k], we[k], preferred_element_type=jnp.float32) for k in range(nz)]
    )
    ys = []
    for s in (2, 1, 3):
        ys.append(go(remote(part.at[y], part.at[y], y_s.at[s - 1], y_r.at[s - 1], (i, vy(s)))))
    ring_step(3)
    for s in range(1, nx):
        wp_c[s - 1].wait_recv()
        o = 2 * ((x - s + nx) % nx) + c
        wp_sib.append(
            go(remote(wp.at[o], wp.at[o], wp_s.at[nx - 1 + s], wp_r.at[nx - 1 + s], (sib, v)))
        )
    for cp in wp_sib:
        cp.wait_recv()
    pp = jnp.dot(prow, wp[...].reshape(-1, width), preferred_element_type=jnp.float32)
    pred[...] = pp.astype(jnp.bfloat16).astype(jnp.float32)
    for rel in RELS[1:5]:
        sibs[rel].wait_recv()

    n_lab = labels.shape[1]
    loads[5].wait()
    lab_rows = jnp.broadcast_to(labels[pl.ds(z, 1), :], (n_lab, n_lab)).astype(jnp.float32).T
    lab_rows = jnp.concatenate([lab_rows, jnp.zeros((16, n_lab), jnp.float32)], axis=0)
    lane = lax.broadcasted_iota(jnp.int32, lab_rows.shape, 1)

    def label_part(p):
        zo = (z + RELS[p] + nz) % nz
        gid = (lane + (zo * NY + y) * block_cols).astype(jnp.float32)
        onehot = jnp.where(lab_rows == gid, 1.0, 0.0).astype(jnp.bfloat16)
        return jnp.dot(
            onehot, wt[p * block_cols : (p + 1) * block_cols, :], preferred_element_type=jnp.float32
        )

    lab_acc = [label_part(p) for p in range(5)]
    for cp in ys:
        cp.wait_recv()
    enc[...] = tree(jnp.add, [part[k] for k in range(NY)]).astype(jnp.bfloat16).astype(jnp.float32)

    cells = 8 * frames
    nvoc = nz * block_cols
    n_blocks = wlab.shape[0]

    def make_hidden(kk, dst):
        ev = enc[...]
        for s in range(8):
            h = jnp.tanh(ev + pred[pl.ds(kk * 8 + s, 1), :])
            dst[s * frames : (s + 1) * frames, :] = h.astype(jnp.bfloat16)

    make_hidden(0, hid_a)
    ring_step(4)
    for rel in RELS[5:]:
        sibs[rel].wait_recv()
    lab_acc = tree(jnp.add, lab_acc + [label_part(p) for p in range(5, nz)])
    blank_rows = lab_acc[n_lab + 8 : n_lab + 16, :]
    for k in range(n_blocks):
        both = jnp.concatenate([lab_acc[8 * k : 8 * k + 8, :], blank_rows], axis=0)
        wlab[k] = both.astype(jnp.bfloat16)
    tail_rows = last_a.shape[0] - 16
    head_rows = nvoc - tail_rows
    last_a[0:tail_rows, :] = wt[head_rows:nvoc, :]
    last_b[0:tail_rows, :] = wt[head_rows:nvoc, :]

    sub_r = lax.broadcasted_iota(jnp.int32, (16, cells), 0)
    sub_l = lax.broadcasted_iota(jnp.int32, (16, cells), 1) // frames
    label_mask = sub_r == sub_l

    def multiply(kk, src, last, dst):
        last[tail_rows:, :] = wlab[kk]
        hv = src[...]
        for q in range(0, head_rows, CHUNK):
            dst[q : q + CHUNK, :] = lax.dot_general(
                wt[q : q + CHUNK, :], hv, NT, preferred_element_type=jnp.float32
            )
        dst[head_rows:, :] = lax.dot_general(last[...], hv, NT, preferred_element_type=jnp.float32)

    def reduce_block(g, k, src):
        m = jnp.max(src[0:nvoc, :], axis=0, keepdims=True)
        t = jnp.sum(jnp.exp(src[0:nvoc, :] - m), axis=0, keepdims=True)
        ll = src[nvoc : nvoc + 16, :]
        stat[y, g, 0, pl.ds(k, 1), :] = m + jnp.log(t)
        stat[y, g, 1, pl.ds(k, 1), :] = jnp.sum(
            jnp.where(label_mask, ll, 0.0), axis=0, keepdims=True
        )
        stat[y, g, 2, pl.ds(k, 1), :] = ll[8:9, :]

    sts = []

    def send_stats(g):
        for s in (2, 1, 3):
            idx = g * (NY - 1) + s - 1
            sts.append(
                go(remote(stat.at[y, g], stat.at[y, g], st_s.at[idx], st_r.at[idx], (i, vy(s))))
            )

    make_hidden(1, hid_b)
    multiply(0, hid_a, last_a, lg_a)

    def two_blocks(j, unused, g):
        k = 2 * j
        make_hidden(k + 2, hid_a)
        multiply(k + 1, hid_b, last_b, lg_b)
        reduce_block(g, k - 8 * g, lg_a)
        make_hidden(k + 3, hid_b)
        multiply(k + 2, hid_a, last_a, lg_a)
        reduce_block(g, k + 1 - 8 * g, lg_b)
        return unused

    groups = stat.shape[1]
    for g in range(groups - 1):
        lax.fori_loop(4 * g, 4 * g + 4, functools.partial(two_blocks, g=g), 0)
        send_stats(g)
    reduce_block(groups - 1, 0, lg_a)
    send_stats(groups - 1)
    loads[6].wait()
    loads[7].wait()
    t_len = flen[z]
    u_len = llen[z]

    for cp in sts:
        cp.wait_recv()
    for g in range(stat.shape[1]):
        log_norm = lse([stat[k, g, 0] for k in range(NY)])
        label_lp = tree(jnp.add, [stat[k, g, 1] for k in range(NY)]) - log_norm
        blank_lp = stat[0, g, 2] - log_norm
        for a, val in enumerate((label_lp, blank_lp)):
            for s in range(8):
                h = val[:, 128 * (s // 4) : 128 * (s // 4) + 128]
                if s % 4:
                    h = pltpu.roll(h, 128 - 32 * (s % 4), 1)
                lp[a, pl.ds(64 * g + s, 8, stride=8), :] = h

    lanes = lax.broadcasted_iota(jnp.int32, lp.shape[1:], 1)
    upos = lax.broadcasted_iota(jnp.int32, lp.shape[1:], 0)
    label_lp = lp[0]
    blank_lp = lp[1]
    last = jnp.where((lanes == t_len - 1) & (upos == u_len), blank_lp, 0.0)
    last = jnp.sum(jnp.sum(last, axis=0, keepdims=True), axis=1, keepdims=True)
    label_lp = jnp.where((lanes == t_len - 1) & (upos >= u_len), 0.0, label_lp)
    blank_lp = jnp.where((lanes == t_len - 2) & (upos > u_len), NEG, blank_lp)
    for bit in range(5):
        moves = (lanes >> bit) & 1 == 1
        label_lp = jnp.where(moves, pltpu.roll(label_lp, 1 << bit, 0), label_lp)
        blank_lp = jnp.where(moves, pltpu.roll(blank_lp, 1 << bit, 0), blank_lp)
    lp[0] = label_lp
    lp[1] = jnp.where(lanes == 0, NEG, pltpu.roll(blank_lp, 1, 1))

    n = lp.shape[1]
    for src_ref, dst_ref in ((lp, band2), (band2, band4), (band4, band8)):
        n = n // 2
        lo = [src_ref[k, pl.ds(0, n, stride=2), :] for k in range(src_ref.shape[0])]
        hi = [src_ref[k, pl.ds(1, n, stride=2), :] for k in range(src_ref.shape[0])]
        for k, val in enumerate(compose(lo, hi)):
            dst_ref[k] = val

    lane8 = lax.broadcasted_iota(jnp.int32, (8, 128), 1)
    state0[0] = jnp.where(lane8 == 0, 0.0, NEG)
    state0[1] = jnp.ones((8, 128), jnp.float32)

    def advance(d, state):
        e, m = state
        nb = band8.shape[0]
        terms = [
            (pltpu.roll(e, j, 1) if j else e)
            + jnp.broadcast_to(band8[j, pl.ds(d, 1), :], (8, 128))
            for j in range(nb)
        ]
        top = tree(jnp.maximum, terms)
        m2 = tree(
            jnp.add,
            [(pltpu.roll(m, j, 1) if j else m) * jnp.exp(terms[j] - top) for j in range(nb)],
        )
        return top, m2

    e, m = lax.fori_loop(0, 20, advance, (state0[0], state0[1]), unroll=4)
    val = jnp.where(lane8 == t_len - 1, e + jnp.log(m), 0.0)
    val = jnp.sum(val, axis=1, keepdims=True) + last
    loss = -val / (t_len + u_len).astype(jnp.float32)
    lossbuf[z] = jnp.broadcast_to(loss, (8, 128))
    los = []
    for s in (4, 3, 5, 2, 6, 1, 7):
        los.append(
            go(remote(lossbuf.at[z], lossbuf.at[z], lo_s.at[s - 1], lo_r.at[s - 1], (i, vz(s))))
        )
    for cp in sends[: -len(los)]:
        cp.wait_send()
    for cp in los:
        cp.wait_recv()
    for k in range(nz):
        out[k : k + 1, :] = lossbuf[k, 0:1, :]
    for cp in los:
        cp.wait_send()


def shards(ndp, nv, encoder_rows, predictor_rows, enc_weight, pred_weight, out_weight, flen, llen, labels):
    utts, fr, feat = encoder_rows.shape
    nz = nv // NY
    per, positions, pwidth = predictor_rows.shape
    width = enc_weight.shape[1]
    frames = fr * ndp
    cols = out_weight.shape[1]
    n_blocks = (positions + 7) // 8
    groups = (n_blocks + 7) // 8
    cells = 8 * frames
    xt = jnp.transpose(encoder_rows, (1, 2, 0)).reshape(fr * feat, utts)
    prows = jnp.transpose(predictor_rows, (1, 0, 2)).reshape(positions * per, pwidth)
    vm = pl.BlockSpec(memory_space=pltpu.VMEM)
    hbm = pl.BlockSpec(memory_space=pltpu.HBM)
    dma = pltpu.SemaphoreType.DMA
    bf, f32, i32 = jnp.bfloat16, jnp.float32, jnp.int32
    nx = ndp // 2

    def pair(n):
        return [dma((n,)), dma((n,))]

    res = pl.pallas_call(
        functools.partial(joint_kernel, ndp, nv),
        out_shape=jax.ShapeDtypeStruct((per, 128), f32),
        in_specs=[hbm] * 8,
        out_specs=vm,
        scratch_shapes=[
            pltpu.VMEM(xt.shape, bf),
            pltpu.VMEM(prows.shape, bf),
            pltpu.VMEM(out_weight.shape, bf),
            pltpu.VMEM(labels.shape, i32),
            pltpu.SMEM(flen.shape, i32),
            pltpu.SMEM(llen.shape, i32),
            pltpu.VMEM((ndp, per * fr, feat), bf),
            pltpu.VMEM((ndp, per * fr, feat), bf),
            pltpu.VMEM((nz, frames, feat), bf),
            pltpu.VMEM((nz, frames, feat), bf),
            pltpu.VMEM((ndp, feat, width), bf),
            pltpu.VMEM((ndp, pred_weight.shape[0], width), bf),
            pltpu.VMEM((NY, frames, width), f32),
            pltpu.VMEM((frames, width), f32),
            pltpu.VMEM((8 * n_blocks + 8, width), f32),
            pltpu.VMEM((nz * cols, width), bf),
            pltpu.VMEM((n_blocks, 16, width), bf),
            pltpu.VMEM((cells, width), bf),
            pltpu.VMEM((cells, width), bf),
            pltpu.VMEM((CHUNK + 16, width), bf),
            pltpu.VMEM((CHUNK + 16, width), bf),
            pltpu.VMEM((nz * cols + 16, cells), f32),
            pltpu.VMEM((nz * cols + 16, cells), f32),
            pltpu.VMEM((NY, groups, 3, 8, cells), f32),
            pltpu.VMEM((2, 64 * groups, 128), f32),
            pltpu.VMEM((3, 32 * groups, 128), f32),
            pltpu.VMEM((5, 16 * groups, 128), f32),
            pltpu.VMEM((9, 8 * groups, 128), f32),
            pltpu.VMEM((nz, 8, 128), f32),
            pltpu.VMEM((2, 8, 128), f32),
            dma((8,)),
            *pair(ndp - 1),
            *pair(nz - 1),
            *pair(2 * nx - 1),
            *pair(2 * nx - 1),
            *pair(nz - 1),
            *pair(nz - 1),
            *pair(NY - 1),
            *pair(groups * (NY - 1)),
            *pair(nz - 1),
        ],
        compiler_params=pltpu.CompilerParams(
            collective_id=0, has_side_effects=True, vmem_limit_bytes=60 * 1024 * 1024
        ),
    )(xt, prows, enc_weight, pred_weight, out_weight, flen, llen, labels)
    return res[:, 0]


def solution(mesh):
    return jax.shard_map(
        functools.partial(shards, mesh.shape["dp"], mesh.shape["vocab"]),
        mesh=mesh,
        in_specs=(
            P(None, "dp", "vocab"),
            P("dp", None, None),
            P("dp", None),
            P("dp", None),
            P(None, "vocab"),
            P("dp"),
            P("dp"),
            P("dp", None),
        ),
        out_specs=P("dp"),
        check_vma=False,
    )
```

```python
import functools

import jax
import jax.numpy as jnp
from jax import lax
from jax.experimental import pallas as pl
from jax.experimental.pallas import tpu as pltpu
from jax.sharding import PartitionSpec as P

MESH = pl.DeviceIdType.MESH
NY = 4
NEG = -1e30
FAR_FIRST = (4, 3, 5, 2, 6, 1, 7)
CHUNK = 256
NT = (((1,), (1,)), ((), ()))


RELS = (0, 1, -1, 2, -2, 3, -3, 4)


def lse(terms):
    if len(terms) == 1:
        return terms[0]
    top = functools.reduce(jnp.maximum, terms)
    return top + jnp.log(tree(jnp.add, [jnp.exp(a - top) for a in terms]))


def tree(op, vals):
    vals = list(vals)
    while len(vals) > 1:
        vals = [op(vals[k], vals[k + 1]) if k + 1 < len(vals) else vals[k] for k in range(0, len(vals), 2)]
    return vals[0]


def compose(lo, hi):
    n = len(lo)
    moved = [[pltpu.roll(b, a, 1) if a else b for b in lo] for a in range(n)]
    return [
        lse([hi[a] + moved[a][j - a] for a in range(n) if 0 <= j - a < n]) for j in range(2 * n - 1)
    ]


def joint_kernel(
    ndp,
    nv,
    xt_h,
    prows_h,
    wenc_h,
    wpred_h,
    wout_h,
    flen_h,
    llen_h,
    labels_h,
    out,
    xt,
    prows,
    wout,
    labels,
    flen,
    llen,
    xin,
    bufb,
    xp,
    bufx,
    we,
    wp,
    part,
    enc,
    pred,
    wt,
    wlab,
    hid_a,
    hid_b,
    last_a,
    last_b,
    lab_near_s,
    far_hot,
    lg_a,
    lg_b,
    stat,
    stat2,
    lp,
    band2,
    band4,
    band8,
    lossbuf,
    state0,
    in_s,
    xd_s,
    xd_r,
    xz_s,
    xz_r,
    we_s,
    we_r,
    wp_s,
    wp_r,
    ring_s,
    ring_r,
    sib_s,
    sib_r,
    y_s,
    y_r,
    st_s,
    st_r,
    lo_s,
    lo_r,
):
    nz = nv // NY
    nx = ndp // 2
    i = lax.axis_index("dp")
    v = lax.axis_index("vocab")
    z = v // NY
    y = v % NY
    x = i // 2
    c = i % 2
    sib = 2 * x + (1 - c)
    frames = part.shape[1]
    width = part.shape[2]
    feat = we.shape[1]

    def vz(s):
        return ((z + s + nz) % nz) * NY + y

    def vy(s):
        return z * NY + (y + s) % NY

    barrier = pltpu.get_barrier_semaphore()
    for s in FAR_FIRST:
        pl.semaphore_signal(barrier, inc=1, device_id=(i, vz(s)), device_id_type=MESH)
    for s in range(1, ndp):
        pl.semaphore_signal(barrier, inc=1, device_id=((i + s) % ndp, v), device_id_type=MESH)
    for s in range(1, NY):
        pl.semaphore_signal(barrier, inc=1, device_id=(i, vy(s)), device_id_type=MESH)

    erow = pl.multiple_of(feat * y, 16)
    loads = []
    for k, (src, dst) in enumerate(
        (
            (xt_h, xt),
            (wout_h, wout),
            (wenc_h.at[pl.ds(erow, feat)], we.at[i]),
            (wpred_h, wp.at[i]),
            (prows_h, prows),
            (labels_h, labels),
            (flen_h, flen),
            (llen_h, llen),
        )
    ):
        cp = pltpu.make_async_copy(src, dst, in_s.at[k])
        cp.start()
        loads.append(cp)

    def remote(src, dst, ssem, rsem, dev):
        return pltpu.make_async_remote_copy(
            src_ref=src, dst_ref=dst, send_sem=ssem, recv_sem=rsem, device_id=dev, device_id_type=MESH
        )

    sends = []

    def go(cp):
        cp.start()
        sends.append(cp)
        return cp

    utts = xt.shape[1]
    fr = xt.shape[0] // feat
    mine = utts * fr
    r_io = lax.broadcasted_iota(jnp.int32, (mine, utts), 0)
    u_io = lax.broadcasted_iota(jnp.int32, (mine, utts), 1)
    loads[0].wait()
    moved = None
    for f in range(fr):
        pick = jnp.where(r_io == u_io * fr + f, 1.0, 0.0).astype(jnp.bfloat16)
        one = lax.dot_general(
            pick, xt[f * feat : (f + 1) * feat, :], NT, preferred_element_type=jnp.float32
        )
        moved = one if moved is None else moved + one
    xin[...] = moved.astype(jnp.bfloat16).reshape(xin.shape)
    bufb[i] = xin[i]
    block_cols = wout.shape[1]
    loads[1].wait()
    wt[0:block_cols, :] = wout[...].astype(jnp.float32).T.astype(jnp.bfloat16)
    stat[y, 1] = jnp.zeros(stat.shape[2:], jnp.float32)
    stat2[y] = jnp.zeros(stat2.shape[1:], jnp.float32)
    loads[2].wait()
    loads[3].wait()

    pl.semaphore_wait(barrier, (ndp - 1) + (nz - 1) + (NY - 1))

    xd = []
    for s in range(1, ndp):
        k = (i + s) % ndp
        xd.append(go(remote(xin.at[k], bufb.at[i], xd_s.at[s - 1], xd_r.at[s - 1], (k, v))))

    half = block_cols // 2

    def slot(rel, lo=0, n=half):
        start = RELS.index(rel) * block_cols + c * half + lo
        return wt.at[pl.ds(pl.multiple_of(start, 16), n)]

    def ring_copy(rel, hop, idx, lo=0, n=half):
        to = rel - hop
        to = nz // 2 if abs(to) == nz // 2 else to
        return remote(
            slot(rel, lo, n), slot(to, lo, n), ring_s.at[idx], ring_r.at[idx], (i, vz(hop))
        )

    def sib_copy(rel):
        idx = RELS.index(rel) - 1
        return remote(slot(rel), slot(rel), sib_s.at[idx], sib_r.at[idx], (sib, v))

    ring = {}
    for idx, hop in enumerate((1, -1, 2, -2)):
        ring[-hop] = go(ring_copy(0, hop, idx))
    sibs = {}

    we_c, wp_c = [], []
    for s in range(1, nx):
        dev = (2 * ((x + s) % nx) + c, v)
        we_c.append(go(remote(we.at[i], we.at[i], we_s.at[s - 1], we_r.at[s - 1], dev)))
    we_sib = [go(remote(we.at[i], we.at[i], we_s.at[nx - 1], we_r.at[nx - 1], (sib, v)))]
    for s in range(1, nx):
        dev = (2 * ((x + s) % nx) + c, v)
        wp_c.append(go(remote(wp.at[i], wp.at[i], wp_s.at[s - 1], wp_r.at[s - 1], dev)))
    wp_sib = [go(remote(wp.at[i], wp.at[i], wp_s.at[nx - 1], wp_r.at[nx - 1], (sib, v)))]

    def to_sibling(*rels):
        for rel in rels:
            sibs[rel] = go(sib_copy(rel))

    rows = bufb.shape[0] * bufb.shape[1]
    r_io = lax.broadcasted_iota(jnp.int32, (rows, rows), 0)
    c_io = lax.broadcasted_iota(jnp.int32, (rows, rows), 1)
    src = ((r_io >> 2) & 7) * 32 + (r_io >> 5) * 4 + (r_io & 3)
    perm = jnp.where(src == c_io, 1.0, 0.0).astype(jnp.bfloat16)
    for rel in (1, -1):
        ring[rel].wait_recv()
    to_sibling(1, -1)
    for cp in xd:
        cp.wait_recv()
    moved = jnp.dot(perm, bufb[...].reshape(rows, feat), preferred_element_type=jnp.float32)
    xp[...] = moved.astype(jnp.bfloat16).reshape(xp.shape)
    xz = []
    for s in FAR_FIRST:
        zt = (z + s) % nz
        xz.append(go(remote(xp.at[zt], bufx.at[z], xz_s.at[s - 1], xz_r.at[s - 1], (i, vz(s)))))
    bufx[z] = xp[z]

    quarter = half // 2
    for rel in (2, -2):
        ring[rel].wait_recv()
    ring[-3] = go(ring_copy(-2, 1, 4))
    ring[3] = go(ring_copy(2, -1, 5))
    fours = [go(ring_copy(-2, 2, 6, 0, quarter)), go(ring_copy(2, -2, 7, quarter, quarter))]
    to_sibling(2, -2)

    positions = prows.shape[0] // xin.shape[0]
    upad = pred.shape[0]
    loads[4].wait()
    p_r = lax.broadcasted_iota(jnp.int32, (upad, prows.shape[0]), 0)
    p_c = lax.broadcasted_iota(jnp.int32, (upad, prows.shape[0]), 1)
    pick = jnp.where(p_c == p_r * xin.shape[0] + z, 1.0, 0.0).astype(jnp.bfloat16)
    prow = jnp.dot(pick, prows[...], preferred_element_type=jnp.float32).astype(jnp.bfloat16)

    for s in range(1, nx):
        we_c[s - 1].wait_recv()
        o = 2 * ((x - s + nx) % nx) + c
        we_sib.append(
            go(remote(we.at[o], we.at[o], we_s.at[nx - 1 + s], we_r.at[nx - 1 + s], (sib, v)))
        )
    for cp in xz:
        cp.wait_recv()
    for cp in we_sib:
        cp.wait_recv()
    part[y] = tree(
        jnp.add, [jnp.dot(bufx[k], we[k], preferred_element_type=jnp.float32) for k in range(nz)]
    ).astype(jnp.bfloat16)
    ys = []
    for s in (2, 1, 3):
        ys.append(go(remote(part.at[y], part.at[y], y_s.at[s - 1], y_r.at[s - 1], (i, vy(s)))))
    for rel in (3, -3):
        ring[rel].wait_recv()
    to_sibling(3, -3)
    for s in range(1, nx):
        wp_c[s - 1].wait_recv()
        o = 2 * ((x - s + nx) % nx) + c
        wp_sib.append(
            go(remote(wp.at[o], wp.at[o], wp_s.at[nx - 1 + s], wp_r.at[nx - 1 + s], (sib, v)))
        )
    for cp in wp_sib:
        cp.wait_recv()
    pp = jnp.dot(prow, wp[...].reshape(-1, width), preferred_element_type=jnp.float32)
    pred[...] = pp.astype(jnp.bfloat16).astype(jnp.float32)
    for rel in RELS[1:5]:
        sibs[rel].wait_recv()

    n_lab = labels.shape[1]
    loads[5].wait()
    lab_rows = jnp.broadcast_to(labels[pl.ds(z, 1), :], (n_lab, n_lab)).astype(jnp.float32).T
    lab_rows = jnp.concatenate([lab_rows, jnp.zeros((16, n_lab), jnp.float32)], axis=0)
    lane = lax.broadcasted_iota(jnp.int32, lab_rows.shape, 1)

    def label_hot(p):
        zo = (z + RELS[p] + nz) % nz
        gid = (lane + (zo * NY + y) * block_cols).astype(jnp.float32)
        return jnp.where(lab_rows == gid, 1.0, 0.0).astype(jnp.bfloat16)

    def label_part(p):
        return jnp.dot(
            label_hot(p),
            wt[p * block_cols : (p + 1) * block_cols, :],
            preferred_element_type=jnp.float32,
        )

    cells = 8 * frames
    n_blocks = wlab.shape[0]
    nvoc = nz * block_cols
    near = 5
    lab_near = tree(jnp.add, [label_part(p) for p in range(near)])
    lab_near_s[...] = lab_near
    far_hot[...] = jnp.concatenate([label_hot(p) for p in range(near, nz)], axis=1)
    tail_rows = last_a.shape[0] - 16
    last_a[0:tail_rows, :] = wt[0:tail_rows, :]
    last_b[0:tail_rows, :] = wt[0:tail_rows, :]
    for cp in fours:
        cp.wait_recv()
    to_sibling(4)
    for cp in ys:
        cp.wait_recv()
    enc[...] = tree(jnp.add, [part[k].astype(jnp.float32) for k in range(NY)]).astype(jnp.bfloat16).astype(jnp.float32)

    def make_hidden(kk, dst, n=8):
        ev = enc[...]
        for s in range(n):
            h = jnp.tanh(ev + pred[pl.ds(kk * 8 + s, 1), :])
            dst[s * frames : (s + 1) * frames, :] = h.astype(jnp.bfloat16)

    def multiply(kk, src, last, dst, n=None, lo=None, hi=None):
        n = n or cells
        hv = src[0:n, :]
        for q in range(lo or tail_rows, hi or nvoc, CHUNK):
            dst[q : q + CHUNK, 0:n] = lax.dot_general(
                wt[q : q + CHUNK, :], hv, NT, preferred_element_type=jnp.float32
            )
        if hi is None:
            last[tail_rows:, :] = wlab[kk]
            both = lax.dot_general(last[...], hv, NT, preferred_element_type=jnp.float32)
            dst[0:tail_rows, 0:n] = both[0:tail_rows, :]
            dst[nvoc:, 0:n] = both[tail_rows:, :]

    make_hidden(0, hid_a)
    make_hidden(1, hid_b)
    multiply(0, hid_a, last_a, lg_a, hi=tail_rows + CHUNK)
    for rel in RELS[near:]:
        sibs[rel].wait_recv()
    lab_far = jnp.dot(
        far_hot[...], wt[near * block_cols :, :], preferred_element_type=jnp.float32
    )
    lab_acc = lab_near_s[...] + lab_far
    blank_rows = lab_acc[n_lab + 8 : n_lab + 16, :]
    for k in range(n_blocks):
        both = jnp.concatenate([lab_acc[8 * k : 8 * k + 8, :], blank_rows], axis=0)
        wlab[k] = both.astype(jnp.bfloat16)

    sub_r = lax.broadcasted_iota(jnp.int32, (16, cells), 0)
    sub_l = lax.broadcasted_iota(jnp.int32, (16, cells), 1) // frames
    label_mask = sub_r == sub_l

    def reduce_block(src, n=None):
        n = n or cells
        m = jnp.max(src[0:nvoc, 0:n], axis=0, keepdims=True)
        t = jnp.sum(jnp.exp(src[0:nvoc, 0:n] - m), axis=0, keepdims=True)
        ll = src[nvoc : nvoc + 16, 0:n]
        label = jnp.sum(jnp.where(label_mask[:, 0:n], ll, 0.0), axis=0, keepdims=True)
        return m + jnp.log(t), label, ll[8:9, :]

    def keep(g, k, src):
        for a, val in enumerate(reduce_block(src)):
            stat[y, g, a, pl.ds(k, 1), :] = val

    sts = []

    def send_stats(ref, g):
        for s in (2, 1, 3):
            idx = g * (NY - 1) + s - 1
            sts.append(go(remote(ref, ref, st_s.at[idx], st_r.at[idx], (i, vy(s)))))

    multiply(0, hid_a, last_a, lg_a, lo=tail_rows + CHUNK)

    def two_blocks(j, unused, g):
        k = 2 * j
        make_hidden(k + 2, hid_a)
        multiply(k + 1, hid_b, last_b, lg_b)
        keep(g, k - 8 * g, lg_a)
        make_hidden(k + 3, hid_b)
        multiply(k + 2, hid_a, last_a, lg_a)
        keep(g, k + 1 - 8 * g, lg_b)
        return unused

    lax.fori_loop(0, 4, functools.partial(two_blocks, g=0), 0)
    send_stats(stat.at[y, 0], 0)
    lax.fori_loop(4, 7, functools.partial(two_blocks, g=1), 0)
    lead = 128
    make_hidden(n_blocks - 1, hid_a, lead // frames)
    multiply(n_blocks - 2, hid_b, last_b, lg_b)
    keep(1, n_blocks - 3 - 8, lg_a)
    send_stats(stat.at[y, 1], 1)
    multiply(n_blocks - 1, hid_a, last_a, lg_a, lead)
    for a, val in enumerate(reduce_block(lg_b)):
        stat2[y, 2 * a : 2 * a + 1, :] = val
    for a, val in enumerate(reduce_block(lg_a, lead)):
        stat2[y, 2 * a + 1 : 2 * a + 2, 0:lead] = val
    send_stats(stat2.at[y], 2)
    loads[6].wait()
    loads[7].wait()
    t_len = flen[z]
    u_len = llen[z]

    for cp in sts:
        cp.wait_recv()
    row8 = lax.broadcasted_iota(jnp.int32, stat.shape[3:], 0)

    def rows_of(k, g, a):
        if g == 0:
            return stat[k, 0, a]
        if g == 1:
            return jnp.where(row8 == 7, stat2[k, 2 * a : 2 * a + 1, :], stat[k, 1, a])
        return jnp.where(row8 == 0, stat2[k, 2 * a + 1 : 2 * a + 2, :], 0.0)

    for g in range(3):
        log_norm = lse([rows_of(k, g, 0) for k in range(NY)])
        label_lp = tree(jnp.add, [rows_of(k, g, 1) for k in range(NY)]) - log_norm
        blank_lp = rows_of(0, g, 2) - log_norm
        for a, val in enumerate((label_lp, blank_lp)):
            for s in range(8):
                h = val[:, 128 * (s // 4) : 128 * (s // 4) + 128]
                if s % 4:
                    h = pltpu.roll(h, 128 - 32 * (s % 4), 1)
                lp[a, pl.ds(64 * g + s, 8, stride=8), :] = h

    lanes = lax.broadcasted_iota(jnp.int32, lp.shape[1:], 1)
    upos = lax.broadcasted_iota(jnp.int32, lp.shape[1:], 0)
    label_lp = lp[0]
    blank_lp = lp[1]
    last = jnp.where((lanes == t_len - 1) & (upos == u_len), blank_lp, 0.0)
    last = jnp.sum(jnp.sum(last, axis=0, keepdims=True), axis=1, keepdims=True)
    label_lp = jnp.where((lanes == t_len - 1) & (upos >= u_len), 0.0, label_lp)
    blank_lp = jnp.where((lanes == t_len - 2) & (upos > u_len), NEG, blank_lp)
    for bit in range(5):
        moves = (lanes >> bit) & 1 == 1
        label_lp = jnp.where(moves, pltpu.roll(label_lp, 1 << bit, 0), label_lp)
        blank_lp = jnp.where(moves, pltpu.roll(blank_lp, 1 << bit, 0), blank_lp)
    lp[0] = label_lp
    lp[1] = jnp.where(lanes == 0, NEG, pltpu.roll(blank_lp, 1, 1))

    n = lp.shape[1]
    for src_ref, dst_ref in ((lp, band2), (band2, band4), (band4, band8)):
        n = n // 2
        lo = [src_ref[k, pl.ds(0, n, stride=2), :] for k in range(src_ref.shape[0])]
        hi = [src_ref[k, pl.ds(1, n, stride=2), :] for k in range(src_ref.shape[0])]
        for k, val in enumerate(compose(lo, hi)):
            dst_ref[k] = val

    lane8 = lax.broadcasted_iota(jnp.int32, (8, 128), 1)
    state0[0] = jnp.where(lane8 == 0, 0.0, NEG)
    state0[1] = jnp.ones((8, 128), jnp.float32)

    def advance(d, state):
        e, m = state
        nb = band8.shape[0]
        terms = [
            (pltpu.roll(e, j, 1) if j else e)
            + jnp.broadcast_to(band8[j, pl.ds(d, 1), :], (8, 128))
            for j in range(nb)
        ]
        top = tree(jnp.maximum, terms)
        m2 = tree(
            jnp.add,
            [(pltpu.roll(m, j, 1) if j else m) * jnp.exp(terms[j] - top) for j in range(nb)],
        )
        return top, m2

    e, m = lax.fori_loop(0, 20, advance, (state0[0], state0[1]), unroll=4)
    val = jnp.where(lane8 == t_len - 1, e + jnp.log(m), 0.0)
    val = jnp.sum(val, axis=1, keepdims=True) + last
    loss = -val / (t_len + u_len).astype(jnp.float32)
    lossbuf[z] = jnp.broadcast_to(loss, (8, 128))
    los = []
    for s in FAR_FIRST:
        los.append(
            go(remote(lossbuf.at[z], lossbuf.at[z], lo_s.at[s - 1], lo_r.at[s - 1], (i, vz(s))))
        )
    for cp in sends[: -len(los)]:
        cp.wait_send()
    for cp in los:
        cp.wait_recv()
    for k in range(nz):
        out[k : k + 1, :] = lossbuf[k, 0:1, :]
    for cp in los:
        cp.wait_send()


def shards(ndp, nv, encoder_rows, predictor_rows, enc_weight, pred_weight, out_weight, flen, llen, labels):
    utts, fr, feat = encoder_rows.shape
    nz = nv // NY
    per, positions, pwidth = predictor_rows.shape
    width = enc_weight.shape[1]
    frames = fr * ndp
    cols = out_weight.shape[1]
    n_blocks = (positions + 7) // 8
    groups = (n_blocks + 7) // 8
    cells = 8 * frames
    xt = jnp.transpose(encoder_rows, (1, 2, 0)).reshape(fr * feat, utts)
    prows = jnp.transpose(predictor_rows, (1, 0, 2)).reshape(positions * per, pwidth)
    vm = pl.BlockSpec(memory_space=pltpu.VMEM)
    hbm = pl.BlockSpec(memory_space=pltpu.HBM)
    dma = pltpu.SemaphoreType.DMA
    bf, f32, i32 = jnp.bfloat16, jnp.float32, jnp.int32
    nx = ndp // 2

    def pair(n):
        return [dma((n,)), dma((n,))]

    res = pl.pallas_call(
        functools.partial(joint_kernel, ndp, nv),
        out_shape=jax.ShapeDtypeStruct((per, 128), f32),
        in_specs=[hbm] * 8,
        out_specs=vm,
        scratch_shapes=[
            pltpu.VMEM(xt.shape, bf),
            pltpu.VMEM(prows.shape, bf),
            pltpu.VMEM(out_weight.shape, bf),
            pltpu.VMEM(labels.shape, i32),
            pltpu.SMEM(flen.shape, i32),
            pltpu.SMEM(llen.shape, i32),
            pltpu.VMEM((ndp, per * fr, feat), bf),
            pltpu.VMEM((ndp, per * fr, feat), bf),
            pltpu.VMEM((nz, frames, feat), bf),
            pltpu.VMEM((nz, frames, feat), bf),
            pltpu.VMEM((ndp, feat, width), bf),
            pltpu.VMEM((ndp, pred_weight.shape[0], width), bf),
            pltpu.VMEM((NY, frames, width), bf),
            pltpu.VMEM((frames, width), f32),
            pltpu.VMEM((8 * n_blocks + 8, width), f32),
            pltpu.VMEM((nz * cols, width), bf),
            pltpu.VMEM((n_blocks, 16, width), bf),
            pltpu.VMEM((cells, width), bf),
            pltpu.VMEM((cells, width), bf),
            pltpu.VMEM((CHUNK + 16, width), bf),
            pltpu.VMEM((CHUNK + 16, width), bf),
            pltpu.VMEM((labels.shape[1] + 16, width), f32),
            pltpu.VMEM((labels.shape[1] + 16, (nz - 5) * cols), bf),
            pltpu.VMEM((nz * cols + 16, cells), f32),
            pltpu.VMEM((nz * cols + 16, cells), f32),
            pltpu.VMEM((NY, groups - 1, 3, 8, cells), f32),
            pltpu.VMEM((NY, 8, cells), f32),
            pltpu.VMEM((2, 64 * groups, 128), f32),
            pltpu.VMEM((3, 32 * groups, 128), f32),
            pltpu.VMEM((5, 16 * groups, 128), f32),
            pltpu.VMEM((9, 8 * groups, 128), f32),
            pltpu.VMEM((nz, 8, 128), f32),
            pltpu.VMEM((2, 8, 128), f32),
            dma((8,)),
            *pair(ndp - 1),
            *pair(nz - 1),
            *pair(2 * nx - 1),
            *pair(2 * nx - 1),
            *pair(nz),
            *pair(nz - 1),
            *pair(NY - 1),
            *pair(groups * (NY - 1)),
            *pair(nz - 1),
        ],
        compiler_params=pltpu.CompilerParams(
            collective_id=0, has_side_effects=True, vmem_limit_bytes=60 * 1024 * 1024
        ),
    )(xt, prows, enc_weight, pred_weight, out_weight, flen, llen, labels)
    return res[:, 0]


def solution(mesh):
    return jax.shard_map(
        functools.partial(shards, mesh.shape["dp"], mesh.shape["vocab"]),
        mesh=mesh,
        in_specs=(
            P(None, "dp", "vocab"),
            P("dp", None, None),
            P("dp", None),
            P("dp", None),
            P(None, "vocab"),
            P("dp"),
            P("dp"),
            P("dp", None),
        ),
        out_specs=P("dp"),
        check_vma=False,
    )
```

```python
import functools

import jax
import jax.numpy as jnp
from jax import lax
from jax.experimental import pallas as pl
from jax.experimental.pallas import tpu as pltpu
from jax.sharding import PartitionSpec as P

MESH = pl.DeviceIdType.MESH
NY = 4
NEG = -1e30
FAR_FIRST = (4, 3, 5, 2, 6, 1, 7)
PRE = 6
NT = (((1,), (1,)), ((), ()))


RELS = (0, 1, -1, 2, -2, 3, -3, 4)


def lse(terms):
    if len(terms) == 1:
        return terms[0]
    top = functools.reduce(jnp.maximum, terms)
    return top + jnp.log(tree(jnp.add, [jnp.exp(a - top) for a in terms]))


def tree(op, vals):
    vals = list(vals)
    while len(vals) > 1:
        vals = [op(vals[k], vals[k + 1]) if k + 1 < len(vals) else vals[k] for k in range(0, len(vals), 2)]
    return vals[0]


def compose(lo, hi):
    n = len(lo)
    moved = [[pltpu.roll(b, a, 1) if a else b for b in lo] for a in range(n)]
    return [
        lse([hi[a] + moved[a][j - a] for a in range(n) if 0 <= j - a < n]) for j in range(2 * n - 1)
    ]


def joint_kernel(
    ndp,
    nv,
    xt_h,
    prows_h,
    wenc_h,
    wpred_h,
    wout_h,
    flen_h,
    llen_h,
    labels_h,
    out,
    xt,
    prows,
    wout,
    labels,
    flen,
    llen,
    xin,
    bufb,
    xp,
    bufx,
    we,
    wp,
    part,
    enc,
    pred,
    wt,
    wlab,
    hid_a,
    hid_b,
    last_a,
    last_b,
    lab_near_s,
    far_hot,
    hid_pre,
    lg_pre,
    lg_a,
    lg_b,
    stat,
    stat2,
    lp,
    band2,
    band4,
    band8,
    lossbuf,
    state0,
    in_s,
    xd_s,
    xd_r,
    xz_s,
    xz_r,
    we_s,
    we_r,
    wp_s,
    wp_r,
    ring_s,
    ring_r,
    sib_s,
    sib_r,
    y_s,
    y_r,
    st_s,
    st_r,
    lo_s,
    lo_r,
):
    nz = nv // NY
    nx = ndp // 2
    i = lax.axis_index("dp")
    v = lax.axis_index("vocab")
    z = v // NY
    y = v % NY
    x = i // 2
    c = i % 2
    sib = 2 * x + (1 - c)
    frames = part.shape[1]
    width = part.shape[2]
    feat = we.shape[1]

    def vz(s):
        return ((z + s + nz) % nz) * NY + y

    def vy(s):
        return z * NY + (y + s) % NY

    barrier = pltpu.get_barrier_semaphore()
    for s in FAR_FIRST:
        pl.semaphore_signal(barrier, inc=1, device_id=(i, vz(s)), device_id_type=MESH)
    for s in range(1, ndp):
        pl.semaphore_signal(barrier, inc=1, device_id=((i + s) % ndp, v), device_id_type=MESH)
    for s in range(1, NY):
        pl.semaphore_signal(barrier, inc=1, device_id=(i, vy(s)), device_id_type=MESH)

    erow = pl.multiple_of(feat * y, 16)
    loads = []
    for k, (src, dst) in enumerate(
        (
            (xt_h, xt),
            (wout_h, wout),
            (wenc_h.at[pl.ds(erow, feat)], we.at[i]),
            (wpred_h, wp.at[i]),
            (prows_h, prows),
            (labels_h, labels),
            (flen_h, flen),
            (llen_h, llen),
        )
    ):
        cp = pltpu.make_async_copy(src, dst, in_s.at[k])
        cp.start()
        loads.append(cp)

    def remote(src, dst, ssem, rsem, dev):
        return pltpu.make_async_remote_copy(
            src_ref=src, dst_ref=dst, send_sem=ssem, recv_sem=rsem, device_id=dev, device_id_type=MESH
        )

    sends = []

    def go(cp):
        cp.start()
        sends.append(cp)
        return cp

    utts = xt.shape[1]
    fr = xt.shape[0] // feat
    mine = utts * fr
    r_io = lax.broadcasted_iota(jnp.int32, (mine, utts), 0)
    u_io = lax.broadcasted_iota(jnp.int32, (mine, utts), 1)
    loads[0].wait()
    moved = None
    for f in range(fr):
        pick = jnp.where(r_io == u_io * fr + f, 1.0, 0.0).astype(jnp.bfloat16)
        one = lax.dot_general(
            pick, xt[f * feat : (f + 1) * feat, :], NT, preferred_element_type=jnp.float32
        )
        moved = one if moved is None else moved + one
    xin[...] = moved.astype(jnp.bfloat16).reshape(xin.shape)
    bufb[i] = xin[i]
    block_cols = wout.shape[1]
    loads[1].wait()
    wt[0:block_cols, :] = wout[...].astype(jnp.float32).T.astype(jnp.bfloat16)
    stat[y, 1] = jnp.zeros(stat.shape[2:], jnp.float32)
    stat2[y] = jnp.zeros(stat2.shape[1:], jnp.float32)
    loads[2].wait()
    loads[3].wait()

    pl.semaphore_wait(barrier, (ndp - 1) + (nz - 1) + (NY - 1))

    xd = []
    for s in range(1, ndp):
        k = (i + s) % ndp
        xd.append(go(remote(xin.at[k], bufb.at[i], xd_s.at[s - 1], xd_r.at[s - 1], (k, v))))

    half = block_cols // 2

    def slot(rel, lo=0, n=half):
        start = RELS.index(rel) * block_cols + c * half + lo
        return wt.at[pl.ds(pl.multiple_of(start, 16), n)]

    def ring_copy(rel, hop, idx, lo=0, n=half):
        to = rel - hop
        to = nz // 2 if abs(to) == nz // 2 else to
        return remote(
            slot(rel, lo, n), slot(to, lo, n), ring_s.at[idx], ring_r.at[idx], (i, vz(hop))
        )

    def sib_copy(rel):
        idx = RELS.index(rel) - 1
        return remote(slot(rel), slot(rel), sib_s.at[idx], sib_r.at[idx], (sib, v))

    ring = {}
    for idx, hop in enumerate((1, -1, 2, -2)):
        ring[-hop] = go(ring_copy(0, hop, idx))
    sibs = {}

    we_c, wp_c = [], []
    for s in range(1, nx):
        dev = (2 * ((x + s) % nx) + c, v)
        we_c.append(go(remote(we.at[i], we.at[i], we_s.at[s - 1], we_r.at[s - 1], dev)))
    we_sib = [go(remote(we.at[i], we.at[i], we_s.at[nx - 1], we_r.at[nx - 1], (sib, v)))]
    for s in range(1, nx):
        dev = (2 * ((x + s) % nx) + c, v)
        wp_c.append(go(remote(wp.at[i], wp.at[i], wp_s.at[s - 1], wp_r.at[s - 1], dev)))
    wp_sib = [go(remote(wp.at[i], wp.at[i], wp_s.at[nx - 1], wp_r.at[nx - 1], (sib, v)))]

    def to_sibling(*rels):
        for rel in rels:
            sibs[rel] = go(sib_copy(rel))

    rows = bufb.shape[0] * bufb.shape[1]
    r_io = lax.broadcasted_iota(jnp.int32, (rows, rows), 0)
    c_io = lax.broadcasted_iota(jnp.int32, (rows, rows), 1)
    src = ((r_io >> 2) & 7) * 32 + (r_io >> 5) * 4 + (r_io & 3)
    perm = jnp.where(src == c_io, 1.0, 0.0).astype(jnp.bfloat16)
    for rel in (1, -1):
        ring[rel].wait_recv()
    to_sibling(1, -1)
    for cp in xd:
        cp.wait_recv()
    moved = jnp.dot(perm, bufb[...].reshape(rows, feat), preferred_element_type=jnp.float32)
    xp[...] = moved.astype(jnp.bfloat16).reshape(xp.shape)
    xz = []
    for s in FAR_FIRST:
        zt = (z + s) % nz
        xz.append(go(remote(xp.at[zt], bufx.at[z], xz_s.at[s - 1], xz_r.at[s - 1], (i, vz(s)))))
    bufx[z] = xp[z]

    quarter = half // 2
    for rel in (2, -2):
        ring[rel].wait_recv()
    ring[-3] = go(ring_copy(-2, 1, 4))
    ring[3] = go(ring_copy(2, -1, 5))
    fours = [go(ring_copy(-2, 2, 6, 0, quarter)), go(ring_copy(2, -2, 7, quarter, quarter))]
    to_sibling(2, -2)

    positions = prows.shape[0] // xin.shape[0]
    upad = pred.shape[0]
    loads[4].wait()
    p_r = lax.broadcasted_iota(jnp.int32, (upad, prows.shape[0]), 0)
    p_c = lax.broadcasted_iota(jnp.int32, (upad, prows.shape[0]), 1)
    pick = jnp.where(p_c == p_r * xin.shape[0] + z, 1.0, 0.0).astype(jnp.bfloat16)
    prow = jnp.dot(pick, prows[...], preferred_element_type=jnp.float32).astype(jnp.bfloat16)

    for s in range(1, nx):
        we_c[s - 1].wait_recv()
        o = 2 * ((x - s + nx) % nx) + c
        we_sib.append(
            go(remote(we.at[o], we.at[o], we_s.at[nx - 1 + s], we_r.at[nx - 1 + s], (sib, v)))
        )
    for cp in xz:
        cp.wait_recv()
    for cp in we_sib:
        cp.wait_recv()
    part[y] = tree(
        jnp.add, [jnp.dot(bufx[k], we[k], preferred_element_type=jnp.float32) for k in range(nz)]
    ).astype(jnp.bfloat16)
    ys = []
    for s in (2, 1, 3):
        ys.append(go(remote(part.at[y], part.at[y], y_s.at[s - 1], y_r.at[s - 1], (i, vy(s)))))
    for rel in (3, -3):
        ring[rel].wait_recv()
    to_sibling(3, -3)
    for s in range(1, nx):
        wp_c[s - 1].wait_recv()
        o = 2 * ((x - s + nx) % nx) + c
        wp_sib.append(
            go(remote(wp.at[o], wp.at[o], wp_s.at[nx - 1 + s], wp_r.at[nx - 1 + s], (sib, v)))
        )
    for cp in wp_sib:
        cp.wait_recv()
    pp = jnp.dot(prow, wp[...].reshape(-1, width), preferred_element_type=jnp.float32)
    pred[...] = pp.astype(jnp.bfloat16).astype(jnp.float32)
    for rel in RELS[1:5]:
        sibs[rel].wait_recv()

    n_lab = labels.shape[1]
    loads[5].wait()
    lab_rows = jnp.broadcast_to(labels[pl.ds(z, 1), :], (n_lab, n_lab)).astype(jnp.float32).T
    lab_rows = jnp.concatenate([lab_rows, jnp.zeros((16, n_lab), jnp.float32)], axis=0)
    lane = lax.broadcasted_iota(jnp.int32, lab_rows.shape, 1)

    def label_hot(p):
        zo = (z + RELS[p] + nz) % nz
        gid = (lane + (zo * NY + y) * block_cols).astype(jnp.float32)
        return jnp.where(lab_rows == gid, 1.0, 0.0).astype(jnp.bfloat16)

    def label_part(p):
        return jnp.dot(
            label_hot(p),
            wt[p * block_cols : (p + 1) * block_cols, :],
            preferred_element_type=jnp.float32,
        )

    cells = 8 * frames
    n_blocks = wlab.shape[0]
    nvoc = nz * block_cols
    near = 5
    lab_near = tree(jnp.add, [label_part(p) for p in range(near)])
    lab_near_s[...] = lab_near
    far_hot[...] = jnp.concatenate([label_hot(p) for p in range(near, nz)], axis=1)
    near_rows = near * block_cols
    far_rows = nvoc - near_rows
    for cp in fours:
        cp.wait_recv()
    to_sibling(4)
    for cp in ys:
        cp.wait_recv()
    enc[...] = tree(jnp.add, [part[k].astype(jnp.float32) for k in range(NY)]).astype(jnp.bfloat16).astype(jnp.float32)

    def make_hidden(kk, dst, n=8):
        ev = enc[...]
        for s in range(n):
            h = jnp.tanh(ev + pred[pl.ds(kk * 8 + s, 1), :])
            dst[s * frames : (s + 1) * frames, :] = h.astype(jnp.bfloat16)

    def multiply_near(src, dst, n=None):
        n = n or cells
        hv = src[0:n, :]
        first = 2 * block_cols
        for lo, hi in ((0, first), (first, near_rows)):
            dst[lo:hi, 0:n] = lax.dot_general(
                wt[lo:hi, :], hv, NT, preferred_element_type=jnp.float32
            )

    def multiply_far(kk, src, last, dst, n=None):
        n = n or cells
        last[far_rows:, :] = wlab[kk]
        dst[near_rows:, 0:n] = lax.dot_general(
            last[...], src[0:n, :], NT, preferred_element_type=jnp.float32
        )

    def multiply(kk, src, last, dst, n=None):
        multiply_near(src, dst, n)
        multiply_far(kk, src, last, dst, n)

    for k in range(PRE):
        make_hidden(k, hid_pre.at[k])
        multiply_near(hid_pre.at[k], lg_pre.at[k])
    make_hidden(PRE, hid_a)
    for rel in RELS[near:]:
        sibs[rel].wait_recv()
    lab_far = jnp.dot(
        far_hot[...], wt[near * block_cols :, :], preferred_element_type=jnp.float32
    )
    lab_acc = lab_near_s[...] + lab_far
    blank_rows = lab_acc[n_lab + 8 : n_lab + 16, :]
    for k in range(n_blocks):
        both = jnp.concatenate([lab_acc[8 * k : 8 * k + 8, :], blank_rows], axis=0)
        wlab[k] = both.astype(jnp.bfloat16)
    last_a[0:far_rows, :] = wt[near_rows:, :]
    last_b[0:far_rows, :] = wt[near_rows:, :]

    sub_r = lax.broadcasted_iota(jnp.int32, (16, cells), 0)
    sub_l = lax.broadcasted_iota(jnp.int32, (16, cells), 1) // frames
    label_mask = sub_r == sub_l

    def reduce_block(src, n=None):
        n = n or cells
        m = jnp.max(src[0:nvoc, 0:n], axis=0, keepdims=True)
        t = jnp.sum(jnp.exp(src[0:nvoc, 0:n] - m), axis=0, keepdims=True)
        ll = src[nvoc : nvoc + 16, 0:n]
        label = jnp.sum(jnp.where(label_mask[:, 0:n], ll, 0.0), axis=0, keepdims=True)
        return m + jnp.log(t), label, ll[8:9, :]

    def keep(g, k, src):
        for a, val in enumerate(reduce_block(src)):
            stat[y, g, a, pl.ds(k, 1), :] = val

    sts = []

    def send_stats(ref, g):
        for s in (2, 1, 3):
            idx = g * (NY - 1) + s - 1
            sts.append(go(remote(ref, ref, st_s.at[idx], st_r.at[idx], (i, vy(s)))))

    for k in range(PRE):
        multiply_far(k, hid_pre.at[k], last_b if k % 2 else last_a, lg_pre.at[k])
        if k:
            keep(0, k - 1, lg_pre.at[k - 1])
    make_hidden(PRE + 1, hid_b)
    multiply(PRE, hid_a, last_a, lg_a)
    keep(0, PRE - 1, lg_pre.at[PRE - 1])

    def two_blocks(j, unused, g):
        k = 2 * j
        make_hidden(k + 2, hid_a)
        multiply(k + 1, hid_b, last_b, lg_b)
        keep(g, k - 8 * g, lg_a)
        make_hidden(k + 3, hid_b)
        multiply(k + 2, hid_a, last_a, lg_a)
        keep(g, k + 1 - 8 * g, lg_b)
        return unused

    lax.fori_loop(PRE // 2, 4, functools.partial(two_blocks, g=0), 0)
    send_stats(stat.at[y, 0], 0)
    lax.fori_loop(4, 7, functools.partial(two_blocks, g=1), 0)
    lead = 128
    make_hidden(n_blocks - 1, hid_a, lead // frames)
    multiply(n_blocks - 2, hid_b, last_b, lg_b)
    keep(1, n_blocks - 3 - 8, lg_a)
    send_stats(stat.at[y, 1], 1)
    multiply(n_blocks - 1, hid_a, last_a, lg_a, lead)
    for a, val in enumerate(reduce_block(lg_b)):
        stat2[y, 2 * a : 2 * a + 1, :] = val
    for a, val in enumerate(reduce_block(lg_a, lead)):
        stat2[y, 2 * a + 1 : 2 * a + 2, 0:lead] = val
    send_stats(stat2.at[y], 2)
    loads[6].wait()
    loads[7].wait()
    t_len = flen[z]
    u_len = llen[z]

    for cp in sts:
        cp.wait_recv()
    row8 = lax.broadcasted_iota(jnp.int32, stat.shape[3:], 0)

    def rows_of(k, g, a):
        if g == 0:
            return stat[k, 0, a]
        if g == 1:
            return jnp.where(row8 == 7, stat2[k, 2 * a : 2 * a + 1, :], stat[k, 1, a])
        return jnp.where(row8 == 0, stat2[k, 2 * a + 1 : 2 * a + 2, :], 0.0)

    for g in range(3):
        log_norm = lse([rows_of(k, g, 0) for k in range(NY)])
        label_lp = tree(jnp.add, [rows_of(k, g, 1) for k in range(NY)]) - log_norm
        blank_lp = rows_of(0, g, 2) - log_norm
        for a, val in enumerate((label_lp, blank_lp)):
            for s in range(8):
                h = val[:, 128 * (s // 4) : 128 * (s // 4) + 128]
                if s % 4:
                    h = pltpu.roll(h, 128 - 32 * (s % 4), 1)
                lp[a, pl.ds(64 * g + s, 8, stride=8), :] = h

    lanes = lax.broadcasted_iota(jnp.int32, lp.shape[1:], 1)
    upos = lax.broadcasted_iota(jnp.int32, lp.shape[1:], 0)
    label_lp = lp[0]
    blank_lp = lp[1]
    last = jnp.where((lanes == t_len - 1) & (upos == u_len), blank_lp, 0.0)
    last = jnp.sum(jnp.sum(last, axis=0, keepdims=True), axis=1, keepdims=True)
    label_lp = jnp.where((lanes == t_len - 1) & (upos >= u_len), 0.0, label_lp)
    blank_lp = jnp.where((lanes == t_len - 2) & (upos > u_len), NEG, blank_lp)
    for bit in range(5):
        moves = (lanes >> bit) & 1 == 1
        label_lp = jnp.where(moves, pltpu.roll(label_lp, 1 << bit, 0), label_lp)
        blank_lp = jnp.where(moves, pltpu.roll(blank_lp, 1 << bit, 0), blank_lp)
    lp[0] = label_lp
    lp[1] = jnp.where(lanes == 0, NEG, pltpu.roll(blank_lp, 1, 1))

    n = lp.shape[1]
    for src_ref, dst_ref in ((lp, band2), (band2, band4), (band4, band8)):
        n = n // 2
        lo = [src_ref[k, pl.ds(0, n, stride=2), :] for k in range(src_ref.shape[0])]
        hi = [src_ref[k, pl.ds(1, n, stride=2), :] for k in range(src_ref.shape[0])]
        for k, val in enumerate(compose(lo, hi)):
            dst_ref[k] = val

    lane8 = lax.broadcasted_iota(jnp.int32, (8, 128), 1)
    state0[0] = jnp.where(lane8 == 0, 0.0, NEG)
    state0[1] = jnp.ones((8, 128), jnp.float32)

    def advance(d, state):
        e, m = state
        nb = band8.shape[0]
        terms = [
            (pltpu.roll(e, j, 1) if j else e)
            + jnp.broadcast_to(band8[j, pl.ds(d, 1), :], (8, 128))
            for j in range(nb)
        ]
        top = tree(jnp.maximum, terms)
        m2 = tree(
            jnp.add,
            [(pltpu.roll(m, j, 1) if j else m) * jnp.exp(terms[j] - top) for j in range(nb)],
        )
        return top, m2

    e, m = lax.fori_loop(0, 20, advance, (state0[0], state0[1]), unroll=4)
    val = jnp.where(lane8 == t_len - 1, e + jnp.log(m), 0.0)
    val = jnp.sum(val, axis=1, keepdims=True) + last
    loss = -val / (t_len + u_len).astype(jnp.float32)
    lossbuf[z] = jnp.broadcast_to(loss, (8, 128))
    los = []
    for s in FAR_FIRST:
        los.append(
            go(remote(lossbuf.at[z], lossbuf.at[z], lo_s.at[s - 1], lo_r.at[s - 1], (i, vz(s))))
        )
    for cp in sends[: -len(los)]:
        cp.wait_send()
    for cp in los:
        cp.wait_recv()
    for k in range(nz):
        out[k : k + 1, :] = lossbuf[k, 0:1, :]
    for cp in los:
        cp.wait_send()


def shards(ndp, nv, encoder_rows, predictor_rows, enc_weight, pred_weight, out_weight, flen, llen, labels):
    utts, fr, feat = encoder_rows.shape
    nz = nv // NY
    per, positions, pwidth = predictor_rows.shape
    width = enc_weight.shape[1]
    frames = fr * ndp
    cols = out_weight.shape[1]
    n_blocks = (positions + 7) // 8
    groups = (n_blocks + 7) // 8
    cells = 8 * frames
    xt = jnp.transpose(encoder_rows, (1, 2, 0)).reshape(fr * feat, utts)
    prows = jnp.transpose(predictor_rows, (1, 0, 2)).reshape(positions * per, pwidth)
    vm = pl.BlockSpec(memory_space=pltpu.VMEM)
    hbm = pl.BlockSpec(memory_space=pltpu.HBM)
    dma = pltpu.SemaphoreType.DMA
    bf, f32, i32 = jnp.bfloat16, jnp.float32, jnp.int32
    nx = ndp // 2

    def pair(n):
        return [dma((n,)), dma((n,))]

    res = pl.pallas_call(
        functools.partial(joint_kernel, ndp, nv),
        out_shape=jax.ShapeDtypeStruct((per, 128), f32),
        in_specs=[hbm] * 8,
        out_specs=vm,
        scratch_shapes=[
            pltpu.VMEM(xt.shape, bf),
            pltpu.VMEM(prows.shape, bf),
            pltpu.VMEM(out_weight.shape, bf),
            pltpu.VMEM(labels.shape, i32),
            pltpu.SMEM(flen.shape, i32),
            pltpu.SMEM(llen.shape, i32),
            pltpu.VMEM((ndp, per * fr, feat), bf),
            pltpu.VMEM((ndp, per * fr, feat), bf),
            pltpu.VMEM((nz, frames, feat), bf),
            pltpu.VMEM((nz, frames, feat), bf),
            pltpu.VMEM((ndp, feat, width), bf),
            pltpu.VMEM((ndp, pred_weight.shape[0], width), bf),
            pltpu.VMEM((NY, frames, width), bf),
            pltpu.VMEM((frames, width), f32),
            pltpu.VMEM((8 * n_blocks + 8, width), f32),
            pltpu.VMEM((nz * cols, width), bf),
            pltpu.VMEM((n_blocks, 16, width), bf),
            pltpu.VMEM((cells, width), bf),
            pltpu.VMEM((cells, width), bf),
            pltpu.VMEM((3 * cols + 16, width), bf),
            pltpu.VMEM((3 * cols + 16, width), bf),
            pltpu.VMEM((labels.shape[1] + 16, width), f32),
            pltpu.VMEM((labels.shape[1] + 16, (nz - 5) * cols), bf),
            pltpu.VMEM((PRE, cells, width), bf),
            pltpu.VMEM((PRE, nz * cols + 16, cells), f32),
            pltpu.VMEM((nz * cols + 16, cells), f32),
            pltpu.VMEM((nz * cols + 16, cells), f32),
            pltpu.VMEM((NY, groups - 1, 3, 8, cells), f32),
            pltpu.VMEM((NY, 8, cells), f32),
            pltpu.VMEM((2, 64 * groups, 128), f32),
            pltpu.VMEM((3, 32 * groups, 128), f32),
            pltpu.VMEM((5, 16 * groups, 128), f32),
            pltpu.VMEM((9, 8 * groups, 128), f32),
            pltpu.VMEM((nz, 8, 128), f32),
            pltpu.VMEM((2, 8, 128), f32),
            dma((8,)),
            *pair(ndp - 1),
            *pair(nz - 1),
            *pair(2 * nx - 1),
            *pair(2 * nx - 1),
            *pair(nz),
            *pair(nz - 1),
            *pair(NY - 1),
            *pair(groups * (NY - 1)),
            *pair(nz - 1),
        ],
        compiler_params=pltpu.CompilerParams(
            collective_id=0, has_side_effects=True, vmem_limit_bytes=60 * 1024 * 1024
        ),
    )(xt, prows, enc_weight, pred_weight, out_weight, flen, llen, labels)
    return res[:, 0]


def solution(mesh):
    return jax.shard_map(
        functools.partial(shards, mesh.shape["dp"], mesh.shape["vocab"]),
        mesh=mesh,
        in_specs=(
            P(None, "dp", "vocab"),
            P("dp", None, None),
            P("dp", None),
            P("dp", None),
            P(None, "vocab"),
            P("dp"),
            P("dp"),
            P("dp", None),
        ),
        out_specs=P("dp"),
        check_vma=False,
    )
```

```python
import functools

import jax
import jax.numpy as jnp
from jax import lax
from jax.experimental import pallas as pl
from jax.experimental.pallas import tpu as pltpu
from jax.sharding import PartitionSpec as P

MESH = pl.DeviceIdType.MESH
NY = 4
NEG = -1e30
FAR_FIRST = (4, 3, 5, 2, 6, 1, 7)
PRE = 8
NT = (((1,), (1,)), ((), ()))


RELS = (0, 1, -1, 2, -2, 3, -3, 4)


def lse(terms):
    if len(terms) == 1:
        return terms[0]
    top = functools.reduce(jnp.maximum, terms)
    return top + jnp.log(tree(jnp.add, [jnp.exp(a - top) for a in terms]))


def tree(op, vals):
    vals = list(vals)
    while len(vals) > 1:
        vals = [op(vals[k], vals[k + 1]) if k + 1 < len(vals) else vals[k] for k in range(0, len(vals), 2)]
    return vals[0]


def compose(lo, hi):
    n = len(lo)
    moved = [[pltpu.roll(b, a, 1) if a else b for b in lo] for a in range(n)]
    return [
        lse([hi[a] + moved[a][j - a] for a in range(n) if 0 <= j - a < n]) for j in range(2 * n - 1)
    ]


def joint_kernel(
    ndp,
    nv,
    xt_h,
    prows_h,
    wenc_h,
    wpred_h,
    wout_h,
    flen_h,
    llen_h,
    labels_h,
    out,
    xt,
    prows,
    wout,
    labels,
    flen,
    llen,
    xin,
    bufb,
    xp,
    bufx,
    we,
    wp,
    part,
    enc,
    pred,
    wt,
    wlab,
    hid_a,
    hid_b,
    last_a,
    last_b,
    lab_near_s,
    far_hot,
    hid_pre,
    lg_pre,
    lg_a,
    lg_b,
    stat,
    stat2,
    lp,
    band2,
    band4,
    band8,
    lossbuf,
    state0,
    in_s,
    xd_s,
    xd_r,
    xz_s,
    xz_r,
    we_s,
    we_r,
    wp_s,
    wp_r,
    ring_s,
    ring_r,
    sib_s,
    sib_r,
    y_s,
    y_r,
    st_s,
    st_r,
    lo_s,
    lo_r,
):
    nz = nv // NY
    nx = ndp // 2
    i = lax.axis_index("dp")
    v = lax.axis_index("vocab")
    z = v // NY
    y = v % NY
    x = i // 2
    c = i % 2
    sib = 2 * x + (1 - c)
    frames = part.shape[1]
    width = part.shape[2]
    feat = we.shape[1]

    def vz(s):
        return ((z + s + nz) % nz) * NY + y

    def vy(s):
        return z * NY + (y + s) % NY

    barrier = pltpu.get_barrier_semaphore()
    for s in FAR_FIRST:
        pl.semaphore_signal(barrier, inc=1, device_id=(i, vz(s)), device_id_type=MESH)
    for s in range(1, ndp):
        pl.semaphore_signal(barrier, inc=1, device_id=((i + s) % ndp, v), device_id_type=MESH)
    for s in range(1, NY):
        pl.semaphore_signal(barrier, inc=1, device_id=(i, vy(s)), device_id_type=MESH)

    erow = pl.multiple_of(feat * y, 16)
    loads = []
    for k, (src, dst) in enumerate(
        (
            (xt_h, xt),
            (wout_h, wout),
            (wenc_h.at[pl.ds(erow, feat)], we.at[i]),
            (wpred_h, wp.at[i]),
            (prows_h, prows),
            (labels_h, labels),
            (flen_h, flen),
            (llen_h, llen),
        )
    ):
        cp = pltpu.make_async_copy(src, dst, in_s.at[k])
        cp.start()
        loads.append(cp)

    def remote(src, dst, ssem, rsem, dev):
        return pltpu.make_async_remote_copy(
            src_ref=src, dst_ref=dst, send_sem=ssem, recv_sem=rsem, device_id=dev, device_id_type=MESH
        )

    sends = []

    def go(cp):
        cp.start()
        sends.append(cp)
        return cp

    utts = xt.shape[1]
    fr = xt.shape[0] // feat
    mine = utts * fr
    r_io = lax.broadcasted_iota(jnp.int32, (mine, utts), 0)
    u_io = lax.broadcasted_iota(jnp.int32, (mine, utts), 1)
    loads[0].wait()
    moved = None
    for f in range(fr):
        pick = jnp.where(r_io == u_io * fr + f, 1.0, 0.0).astype(jnp.bfloat16)
        one = lax.dot_general(
            pick, xt[f * feat : (f + 1) * feat, :], NT, preferred_element_type=jnp.float32
        )
        moved = one if moved is None else moved + one
    xin[...] = moved.astype(jnp.bfloat16).reshape(xin.shape)
    bufb[i] = xin[i]
    block_cols = wout.shape[1]
    loads[1].wait()
    wt[0:block_cols, :] = wout[...].astype(jnp.float32).T.astype(jnp.bfloat16)
    stat[y, 1] = jnp.zeros(stat.shape[2:], jnp.float32)
    stat2[y] = jnp.zeros(stat2.shape[1:], jnp.float32)
    loads[2].wait()
    loads[3].wait()

    pl.semaphore_wait(barrier, (ndp - 1) + (nz - 1) + (NY - 1))

    xd = []
    for s in range(1, ndp):
        k = (i + s) % ndp
        xd.append(go(remote(xin.at[k], bufb.at[i], xd_s.at[s - 1], xd_r.at[s - 1], (k, v))))

    half = block_cols // 2

    def slot(rel, lo=0, n=half):
        start = RELS.index(rel) * block_cols + c * half + lo
        return wt.at[pl.ds(pl.multiple_of(start, 16), n)]

    def ring_copy(rel, hop, idx, lo=0, n=half):
        to = rel - hop
        to = nz // 2 if abs(to) == nz // 2 else to
        return remote(
            slot(rel, lo, n), slot(to, lo, n), ring_s.at[idx], ring_r.at[idx], (i, vz(hop))
        )

    def sib_copy(rel):
        idx = RELS.index(rel) - 1
        return remote(slot(rel), slot(rel), sib_s.at[idx], sib_r.at[idx], (sib, v))

    ring = {}
    for idx, hop in enumerate((1, -1, 2, -2)):
        ring[-hop] = go(ring_copy(0, hop, idx))
    sibs = {}

    we_c, wp_c = [], []
    for s in range(1, nx):
        dev = (2 * ((x + s) % nx) + c, v)
        we_c.append(go(remote(we.at[i], we.at[i], we_s.at[s - 1], we_r.at[s - 1], dev)))
    we_sib = [go(remote(we.at[i], we.at[i], we_s.at[nx - 1], we_r.at[nx - 1], (sib, v)))]
    for s in range(1, nx):
        dev = (2 * ((x + s) % nx) + c, v)
        wp_c.append(go(remote(wp.at[i], wp.at[i], wp_s.at[s - 1], wp_r.at[s - 1], dev)))
    wp_sib = [go(remote(wp.at[i], wp.at[i], wp_s.at[nx - 1], wp_r.at[nx - 1], (sib, v)))]

    def to_sibling(*rels):
        for rel in rels:
            sibs[rel] = go(sib_copy(rel))

    rows = bufb.shape[0] * bufb.shape[1]
    r_io = lax.broadcasted_iota(jnp.int32, (rows, rows), 0)
    c_io = lax.broadcasted_iota(jnp.int32, (rows, rows), 1)
    src = ((r_io >> 2) & 7) * 32 + (r_io >> 5) * 4 + (r_io & 3)
    perm = jnp.where(src == c_io, 1.0, 0.0).astype(jnp.bfloat16)
    for rel in (1, -1):
        ring[rel].wait_recv()
    to_sibling(1, -1)
    for cp in xd:
        cp.wait_recv()
    moved = jnp.dot(perm, bufb[...].reshape(rows, feat), preferred_element_type=jnp.float32)
    xp[...] = moved.astype(jnp.bfloat16).reshape(xp.shape)
    xz = []
    for s in FAR_FIRST:
        zt = (z + s) % nz
        xz.append(go(remote(xp.at[zt], bufx.at[z], xz_s.at[s - 1], xz_r.at[s - 1], (i, vz(s)))))
    bufx[z] = xp[z]

    quarter = half // 2
    for rel in (2, -2):
        ring[rel].wait_recv()
    ring[-3] = go(ring_copy(-2, 1, 4))
    ring[3] = go(ring_copy(2, -1, 5))
    fours = [go(ring_copy(-2, 2, 6, 0, quarter)), go(ring_copy(2, -2, 7, quarter, quarter))]
    to_sibling(2, -2)

    positions = prows.shape[0] // xin.shape[0]
    upad = pred.shape[0]
    loads[4].wait()
    p_r = lax.broadcasted_iota(jnp.int32, (upad, prows.shape[0]), 0)
    p_c = lax.broadcasted_iota(jnp.int32, (upad, prows.shape[0]), 1)
    pick = jnp.where(p_c == p_r * xin.shape[0] + z, 1.0, 0.0).astype(jnp.bfloat16)
    prow = jnp.dot(pick, prows[...], preferred_element_type=jnp.float32).astype(jnp.bfloat16)

    for s in range(1, nx):
        we_c[s - 1].wait_recv()
        o = 2 * ((x - s + nx) % nx) + c
        we_sib.append(
            go(remote(we.at[o], we.at[o], we_s.at[nx - 1 + s], we_r.at[nx - 1 + s], (sib, v)))
        )
    for cp in xz:
        cp.wait_recv()
    for cp in we_sib:
        cp.wait_recv()
    part[y] = tree(
        jnp.add, [jnp.dot(bufx[k], we[k], preferred_element_type=jnp.float32) for k in range(nz)]
    ).astype(jnp.bfloat16)
    ys = []
    for s in (2, 1, 3):
        ys.append(go(remote(part.at[y], part.at[y], y_s.at[s - 1], y_r.at[s - 1], (i, vy(s)))))
    for rel in (3, -3):
        ring[rel].wait_recv()
    to_sibling(3, -3)
    for s in range(1, nx):
        wp_c[s - 1].wait_recv()
        o = 2 * ((x - s + nx) % nx) + c
        wp_sib.append(
            go(remote(wp.at[o], wp.at[o], wp_s.at[nx - 1 + s], wp_r.at[nx - 1 + s], (sib, v)))
        )
    for cp in wp_sib:
        cp.wait_recv()
    pp = jnp.dot(prow, wp[...].reshape(-1, width), preferred_element_type=jnp.float32)
    pred[...] = pp.astype(jnp.bfloat16).astype(jnp.float32)
    for rel in RELS[1:5]:
        sibs[rel].wait_recv()

    n_lab = labels.shape[1]
    loads[5].wait()
    lab_rows = jnp.broadcast_to(labels[pl.ds(z, 1), :], (n_lab, n_lab)).astype(jnp.float32).T
    lab_rows = jnp.concatenate([lab_rows, jnp.zeros((16, n_lab), jnp.float32)], axis=0)
    lane = lax.broadcasted_iota(jnp.int32, lab_rows.shape, 1)

    def label_hot(p):
        zo = (z + RELS[p] + nz) % nz
        gid = (lane + (zo * NY + y) * block_cols).astype(jnp.float32)
        return jnp.where(lab_rows == gid, 1.0, 0.0).astype(jnp.bfloat16)

    def label_part(p):
        return jnp.dot(
            label_hot(p),
            wt[p * block_cols : (p + 1) * block_cols, :],
            preferred_element_type=jnp.float32,
        )

    cells = 8 * frames
    n_blocks = wlab.shape[0]
    nvoc = nz * block_cols
    near = 5
    lab_near = tree(jnp.add, [label_part(p) for p in range(near)])
    lab_near_s[...] = lab_near
    far_hot[...] = jnp.concatenate([label_hot(p) for p in range(near, nz)], axis=1)
    near_rows = near * block_cols
    far_rows = nvoc - near_rows
    for cp in fours:
        cp.wait_recv()
    to_sibling(4)
    for cp in ys:
        cp.wait_recv()
    enc[...] = tree(jnp.add, [part[k].astype(jnp.float32) for k in range(NY)]).astype(jnp.bfloat16).astype(jnp.float32)

    def make_hidden(kk, dst, n=8):
        ev = enc[...]
        for s in range(n):
            h = jnp.tanh(ev + pred[pl.ds(kk * 8 + s, 1), :])
            dst[s * frames : (s + 1) * frames, :] = h.astype(jnp.bfloat16)

    def multiply_near(src, dst, n=None):
        n = n or cells
        hv = src[0:n, :]
        first = 2 * block_cols
        for lo, hi in ((0, near_rows),):
            dst[lo:hi, 0:n] = lax.dot_general(
                wt[lo:hi, :], hv, NT, preferred_element_type=jnp.float32
            )

    def multiply_far(kk, src, last, dst, n=None):
        n = n or cells
        last[far_rows:, :] = wlab[kk]
        dst[near_rows:, 0:n] = lax.dot_general(
            last[...], src[0:n, :], NT, preferred_element_type=jnp.float32
        )

    def multiply(kk, src, last, dst, n=None):
        multiply_near(src, dst, n)
        multiply_far(kk, src, last, dst, n)

    for k in range(PRE):
        make_hidden(k, hid_pre.at[k])
        multiply_near(hid_pre.at[k], lg_pre.at[k])
    make_hidden(PRE, hid_a)
    for rel in RELS[near:]:
        sibs[rel].wait_recv()
    lab_far = jnp.dot(
        far_hot[...], wt[near * block_cols :, :], preferred_element_type=jnp.float32
    )
    lab_acc = lab_near_s[...] + lab_far
    blank_rows = lab_acc[n_lab + 8 : n_lab + 16, :]
    for k in range(n_blocks):
        both = jnp.concatenate([lab_acc[8 * k : 8 * k + 8, :], blank_rows], axis=0)
        wlab[k] = both.astype(jnp.bfloat16)
    last_a[0:far_rows, :] = wt[near_rows:, :]
    last_b[0:far_rows, :] = wt[near_rows:, :]

    sub_r = lax.broadcasted_iota(jnp.int32, (16, cells), 0)
    sub_l = lax.broadcasted_iota(jnp.int32, (16, cells), 1) // frames
    label_mask = sub_r == sub_l

    def reduce_block(src, n=None):
        n = n or cells
        m = jnp.max(src[0:nvoc, 0:n], axis=0, keepdims=True)
        t = jnp.sum(jnp.exp(src[0:nvoc, 0:n] - m), axis=0, keepdims=True)
        ll = src[nvoc : nvoc + 16, 0:n]
        label = jnp.sum(jnp.where(label_mask[:, 0:n], ll, 0.0), axis=0, keepdims=True)
        return m + jnp.log(t), label, ll[8:9, :]

    def keep(g, k, src):
        for a, val in enumerate(reduce_block(src)):
            stat[y, g, a, pl.ds(k, 1), :] = val

    sts = []

    def send_stats(ref, g):
        for s in (2, 1, 3):
            idx = g * (NY - 1) + s - 1
            sts.append(go(remote(ref, ref, st_s.at[idx], st_r.at[idx], (i, vy(s)))))

    for k in range(PRE):
        multiply_far(k, hid_pre.at[k], last_b if k % 2 else last_a, lg_pre.at[k])
        if k:
            keep(0, k - 1, lg_pre.at[k - 1])
    make_hidden(PRE + 1, hid_b)
    multiply(PRE, hid_a, last_a, lg_a)
    keep(0, PRE - 1, lg_pre.at[PRE - 1])

    def two_blocks(j, unused, g):
        k = 2 * j
        make_hidden(k + 2, hid_a)
        multiply(k + 1, hid_b, last_b, lg_b)
        keep(g, k - 8 * g, lg_a)
        make_hidden(k + 3, hid_b)
        multiply(k + 2, hid_a, last_a, lg_a)
        keep(g, k + 1 - 8 * g, lg_b)
        return unused

    lax.fori_loop(PRE // 2, 4, functools.partial(two_blocks, g=0), 0)
    send_stats(stat.at[y, 0], 0)
    lax.fori_loop(4, 7, functools.partial(two_blocks, g=1), 0, unroll=3)
    lead = 128
    make_hidden(n_blocks - 1, hid_a, lead // frames)
    multiply(n_blocks - 2, hid_b, last_b, lg_b)
    keep(1, n_blocks - 3 - 8, lg_a)
    send_stats(stat.at[y, 1], 1)
    multiply(n_blocks - 1, hid_a, last_a, lg_a, lead)
    for a, val in enumerate(reduce_block(lg_b)):
        stat2[y, 2 * a : 2 * a + 1, :] = val
    for a, val in enumerate(reduce_block(lg_a, lead)):
        stat2[y, 2 * a + 1 : 2 * a + 2, 0:lead] = val
    send_stats(stat2.at[y], 2)
    loads[6].wait()
    loads[7].wait()
    t_len = flen[z]
    u_len = llen[z]

    for cp in sts:
        cp.wait_recv()
    row8 = lax.broadcasted_iota(jnp.int32, stat.shape[3:], 0)

    def rows_of(k, g, a):
        if g == 0:
            return stat[k, 0, a]
        if g == 1:
            return jnp.where(row8 == 7, stat2[k, 2 * a : 2 * a + 1, :], stat[k, 1, a])
        return jnp.where(row8 == 0, stat2[k, 2 * a + 1 : 2 * a + 2, :], 0.0)

    for g in range(3):
        log_norm = lse([rows_of(k, g, 0) for k in range(NY)])
        label_lp = tree(jnp.add, [rows_of(k, g, 1) for k in range(NY)]) - log_norm
        blank_lp = rows_of(0, g, 2) - log_norm
        for a, val in enumerate((label_lp, blank_lp)):
            for s in range(8):
                h = val[:, 128 * (s // 4) : 128 * (s // 4) + 128]
                if s % 4:
                    h = pltpu.roll(h, 128 - 32 * (s % 4), 1)
                lp[a, pl.ds(64 * g + s, 8, stride=8), :] = h

    lanes = lax.broadcasted_iota(jnp.int32, lp.shape[1:], 1)
    upos = lax.broadcasted_iota(jnp.int32, lp.shape[1:], 0)
    label_lp = lp[0]
    blank_lp = lp[1]
    last = jnp.where((lanes == t_len - 1) & (upos == u_len), blank_lp, 0.0)
    last = jnp.sum(jnp.sum(last, axis=0, keepdims=True), axis=1, keepdims=True)
    label_lp = jnp.where((lanes == t_len - 1) & (upos >= u_len), 0.0, label_lp)
    blank_lp = jnp.where((lanes == t_len - 2) & (upos > u_len), NEG, blank_lp)
    for bit in range(5):
        moves = (lanes >> bit) & 1 == 1
        label_lp = jnp.where(moves, pltpu.roll(label_lp, 1 << bit, 0), label_lp)
        blank_lp = jnp.where(moves, pltpu.roll(blank_lp, 1 << bit, 0), blank_lp)
    lp[0] = label_lp
    lp[1] = jnp.where(lanes == 0, NEG, pltpu.roll(blank_lp, 1, 1))

    n = lp.shape[1]
    for src_ref, dst_ref in ((lp, band2), (band2, band4), (band4, band8)):
        n = n // 2
        lo = [src_ref[k, pl.ds(0, n, stride=2), :] for k in range(src_ref.shape[0])]
        hi = [src_ref[k, pl.ds(1, n, stride=2), :] for k in range(src_ref.shape[0])]
        for k, val in enumerate(compose(lo, hi)):
            dst_ref[k] = val

    lane8 = lax.broadcasted_iota(jnp.int32, (8, 128), 1)
    state0[0] = jnp.where(lane8 == 0, 0.0, NEG)
    state0[1] = jnp.ones((8, 128), jnp.float32)

    def advance(d, state):
        e, m = state
        nb = band8.shape[0]
        terms = [
            (pltpu.roll(e, j, 1) if j else e)
            + jnp.broadcast_to(band8[j, pl.ds(d, 1), :], (8, 128))
            for j in range(nb)
        ]
        top = tree(jnp.maximum, terms)
        m2 = tree(
            jnp.add,
            [(pltpu.roll(m, j, 1) if j else m) * jnp.exp(terms[j] - top) for j in range(nb)],
        )
        return top, m2

    e, m = lax.fori_loop(0, 20, advance, (state0[0], state0[1]), unroll=4)
    val = jnp.where(lane8 == t_len - 1, e + jnp.log(m), 0.0)
    val = jnp.sum(val, axis=1, keepdims=True) + last
    loss = -val / (t_len + u_len).astype(jnp.float32)
    lossbuf[z] = jnp.broadcast_to(loss, (8, 128))
    los = []
    for s in FAR_FIRST:
        los.append(
            go(remote(lossbuf.at[z], lossbuf.at[z], lo_s.at[s - 1], lo_r.at[s - 1], (i, vz(s))))
        )
    for cp in sends[: -len(los)]:
        cp.wait_send()
    for cp in los:
        cp.wait_recv()
    for k in range(nz):
        out[k : k + 1, :] = lossbuf[k, 0:1, :]
    for cp in los:
        cp.wait_send()


def shards(ndp, nv, encoder_rows, predictor_rows, enc_weight, pred_weight, out_weight, flen, llen, labels):
    utts, fr, feat = encoder_rows.shape
    nz = nv // NY
    per, positions, pwidth = predictor_rows.shape
    width = enc_weight.shape[1]
    frames = fr * ndp
    cols = out_weight.shape[1]
    n_blocks = (positions + 7) // 8
    groups = (n_blocks + 7) // 8
    cells = 8 * frames
    xt = jnp.transpose(encoder_rows, (1, 2, 0)).reshape(fr * feat, utts)
    prows = jnp.transpose(predictor_rows, (1, 0, 2)).reshape(positions * per, pwidth)
    vm = pl.BlockSpec(memory_space=pltpu.VMEM)
    hbm = pl.BlockSpec(memory_space=pltpu.HBM)
    dma = pltpu.SemaphoreType.DMA
    bf, f32, i32 = jnp.bfloat16, jnp.float32, jnp.int32
    nx = ndp // 2

    def pair(n):
        return [dma((n,)), dma((n,))]

    res = pl.pallas_call(
        functools.partial(joint_kernel, ndp, nv),
        out_shape=jax.ShapeDtypeStruct((per, 128), f32),
        in_specs=[hbm] * 8,
        out_specs=vm,
        scratch_shapes=[
            pltpu.VMEM(xt.shape, bf),
            pltpu.VMEM(prows.shape, bf),
            pltpu.VMEM(out_weight.shape, bf),
            pltpu.VMEM(labels.shape, i32),
            pltpu.SMEM(flen.shape, i32),
            pltpu.SMEM(llen.shape, i32),
            pltpu.VMEM((ndp, per * fr, feat), bf),
            pltpu.VMEM((ndp, per * fr, feat), bf),
            pltpu.VMEM((nz, frames, feat), bf),
            pltpu.VMEM((nz, frames, feat), bf),
            pltpu.VMEM((ndp, feat, width), bf),
            pltpu.VMEM((ndp, pred_weight.shape[0], width), bf),
            pltpu.VMEM((NY, frames, width), bf),
            pltpu.VMEM((frames, width), f32),
            pltpu.VMEM((8 * n_blocks + 8, width), f32),
            pltpu.VMEM((nz * cols, width), bf),
            pltpu.VMEM((n_blocks, 16, width), bf),
            pltpu.VMEM((cells, width), bf),
            pltpu.VMEM((cells, width), bf),
            pltpu.VMEM((3 * cols + 16, width), bf),
            pltpu.VMEM((3 * cols + 16, width), bf),
            pltpu.VMEM((labels.shape[1] + 16, width), f32),
            pltpu.VMEM((labels.shape[1] + 16, (nz - 5) * cols), bf),
            pltpu.VMEM((PRE, cells, width), bf),
            pltpu.VMEM((PRE, nz * cols + 16, cells), f32),
            pltpu.VMEM((nz * cols + 16, cells), f32),
            pltpu.VMEM((nz * cols + 16, cells), f32),
            pltpu.VMEM((NY, groups - 1, 3, 8, cells), f32),
            pltpu.VMEM((NY, 8, cells), f32),
            pltpu.VMEM((2, 64 * groups, 128), f32),
            pltpu.VMEM((3, 32 * groups, 128), f32),
            pltpu.VMEM((5, 16 * groups, 128), f32),
            pltpu.VMEM((9, 8 * groups, 128), f32),
            pltpu.VMEM((nz, 8, 128), f32),
            pltpu.VMEM((2, 8, 128), f32),
            dma((8,)),
            *pair(ndp - 1),
            *pair(nz - 1),
            *pair(2 * nx - 1),
            *pair(2 * nx - 1),
            *pair(nz),
            *pair(nz - 1),
            *pair(NY - 1),
            *pair(groups * (NY - 1)),
            *pair(nz - 1),
        ],
        compiler_params=pltpu.CompilerParams(
            collective_id=0, has_side_effects=True, vmem_limit_bytes=60 * 1024 * 1024
        ),
    )(xt, prows, enc_weight, pred_weight, out_weight, flen, llen, labels)
    return res[:, 0]


def solution(mesh):
    return jax.shard_map(
        functools.partial(shards, mesh.shape["dp"], mesh.shape["vocab"]),
        mesh=mesh,
        in_specs=(
            P(None, "dp", "vocab"),
            P("dp", None, None),
            P("dp", None),
            P("dp", None),
            P(None, "vocab"),
            P("dp"),
            P("dp"),
            P("dp", None),
        ),
        out_specs=P("dp"),
        check_vma=False,
    )
```

```python
import functools

import jax
import jax.numpy as jnp
from jax import lax
from jax.experimental import pallas as pl
from jax.experimental.pallas import tpu as pltpu
from jax.sharding import PartitionSpec as P

MESH = pl.DeviceIdType.MESH
NY = 4
NEG = -1e30
FAR_FIRST = (4, 3, 5, 2, 6, 1, 7)
PRE = 8
SPARE = 16
NT = (((1,), (1,)), ((), ()))


RELS = (0, 1, -1, 2, -2, 3, -3, 4)


def lse(terms):
    if len(terms) == 1:
        return terms[0]
    top = functools.reduce(jnp.maximum, terms)
    return top + jnp.log(tree(jnp.add, [jnp.exp(a - top) for a in terms]))


def tree(op, vals):
    vals = list(vals)
    while len(vals) > 1:
        vals = [op(vals[k], vals[k + 1]) if k + 1 < len(vals) else vals[k] for k in range(0, len(vals), 2)]
    return vals[0]


def compose(lo, hi):
    n = len(lo)
    moved = [[pltpu.roll(b, a, 1) if a else b for b in lo] for a in range(n)]
    return [
        lse([hi[a] + moved[a][j - a] for a in range(n) if 0 <= j - a < n]) for j in range(2 * n - 1)
    ]


def joint_kernel(
    ndp,
    nv,
    xt_h,
    prows_h,
    wenc_h,
    wpred_h,
    wout_h,
    flen_h,
    llen_h,
    labels_h,
    out,
    xt,
    prows,
    wout,
    labels,
    flen,
    llen,
    xin,
    bufb,
    xp,
    bufx,
    we,
    wp,
    part,
    enc,
    pred,
    wt,
    wlab,
    hid_a,
    hid_b,
    last_a,
    last_b,
    lab_near_s,
    far_hot,
    hid_pre,
    lg_pre,
    lg_a,
    lg_b,
    stat,
    stat2,
    lp,
    band2,
    band4,
    band8,
    lossbuf,
    state0,
    in_s,
    xd_s,
    xd_r,
    xz_s,
    xz_r,
    we_s,
    we_r,
    wp_s,
    wp_r,
    ring_s,
    ring_r,
    sib_s,
    sib_r,
    y_s,
    y_r,
    st_s,
    st_r,
    lo_s,
    lo_r,
):
    nz = nv // NY
    nx = ndp // 2
    i = lax.axis_index("dp")
    v = lax.axis_index("vocab")
    z = v // NY
    y = v % NY
    x = i // 2
    c = i % 2
    sib = 2 * x + (1 - c)
    frames = part.shape[1]
    width = part.shape[2]
    feat = we.shape[1]

    def vz(s):
        return ((z + s + nz) % nz) * NY + y

    def vy(s):
        return z * NY + (y + s) % NY

    barrier = pltpu.get_barrier_semaphore()
    for s in FAR_FIRST:
        pl.semaphore_signal(barrier, inc=1, device_id=(i, vz(s)), device_id_type=MESH)
    for s in range(1, ndp):
        pl.semaphore_signal(barrier, inc=1, device_id=((i + s) % ndp, v), device_id_type=MESH)
    for s in range(1, NY):
        pl.semaphore_signal(barrier, inc=1, device_id=(i, vy(s)), device_id_type=MESH)

    erow = pl.multiple_of(feat * y, 16)
    loads = []
    for k, (src, dst) in enumerate(
        (
            (xt_h, xt),
            (wout_h, wout),
            (wenc_h.at[pl.ds(erow, feat)], we.at[i]),
            (wpred_h, wp.at[i]),
            (prows_h, prows),
            (labels_h, labels.at[pl.ds(0, labels_h.shape[0])]),
            (flen_h, flen),
            (llen_h, llen),
        )
    ):
        cp = pltpu.make_async_copy(src, dst, in_s.at[k])
        cp.start()
        loads.append(cp)

    def remote(src, dst, ssem, rsem, dev):
        return pltpu.make_async_remote_copy(
            src_ref=src, dst_ref=dst, send_sem=ssem, recv_sem=rsem, device_id=dev, device_id_type=MESH
        )

    sends = []

    def go(cp):
        cp.start()
        sends.append(cp)
        return cp

    utts = xt.shape[1]
    fr = xt.shape[0] // feat
    mine = utts * fr
    r_io = lax.broadcasted_iota(jnp.int32, (mine, utts), 0)
    u_io = lax.broadcasted_iota(jnp.int32, (mine, utts), 1)
    loads[0].wait()
    moved = None
    for f in range(fr):
        pick = jnp.where(r_io == u_io * fr + f, 1.0, 0.0).astype(jnp.bfloat16)
        one = lax.dot_general(
            pick, xt[f * feat : (f + 1) * feat, :], NT, preferred_element_type=jnp.float32
        )
        moved = one if moved is None else moved + one
    xin[...] = moved.astype(jnp.bfloat16).reshape(xin.shape)
    bufb[i] = xin[i]
    block_cols = wout.shape[1]
    loads[1].wait()
    wt[0:block_cols, :] = wout[...].astype(jnp.float32).T.astype(jnp.bfloat16)
    stat[y, 1] = jnp.zeros(stat.shape[2:], jnp.float32)
    stat2[y] = jnp.zeros(stat2.shape[1:], jnp.float32)
    loads[2].wait()
    loads[3].wait()

    pl.semaphore_wait(barrier, (ndp - 1) + (nz - 1) + (NY - 1))

    xd = []
    for s in range(1, ndp):
        k = (i + s) % ndp
        xd.append(go(remote(xin.at[k], bufb.at[i], xd_s.at[s - 1], xd_r.at[s - 1], (k, v))))

    half = block_cols // 2

    def slot(rel, lo=0, n=half):
        start = RELS.index(rel) * block_cols + c * half + lo
        return wt.at[pl.ds(pl.multiple_of(start, 16), n)]

    def ring_copy(rel, hop, idx, lo=0, n=half):
        to = rel - hop
        to = nz // 2 if abs(to) == nz // 2 else to
        return remote(
            slot(rel, lo, n), slot(to, lo, n), ring_s.at[idx], ring_r.at[idx], (i, vz(hop))
        )

    def sib_copy(rel):
        idx = RELS.index(rel) - 1
        return remote(slot(rel), slot(rel), sib_s.at[idx], sib_r.at[idx], (sib, v))

    ring = {}
    for idx, hop in enumerate((1, -1, 2, -2)):
        ring[-hop] = go(ring_copy(0, hop, idx))
    sibs = {}

    we_c, wp_c = [], []
    for s in range(1, nx):
        dev = (2 * ((x + s) % nx) + c, v)
        we_c.append(go(remote(we.at[i], we.at[i], we_s.at[s - 1], we_r.at[s - 1], dev)))
    we_sib = [go(remote(we.at[i], we.at[i], we_s.at[nx - 1], we_r.at[nx - 1], (sib, v)))]
    for s in range(1, nx):
        dev = (2 * ((x + s) % nx) + c, v)
        wp_c.append(go(remote(wp.at[i], wp.at[i], wp_s.at[s - 1], wp_r.at[s - 1], dev)))
    wp_sib = [go(remote(wp.at[i], wp.at[i], wp_s.at[nx - 1], wp_r.at[nx - 1], (sib, v)))]

    def to_sibling(*rels):
        for rel in rels:
            sibs[rel] = go(sib_copy(rel))

    rows = bufb.shape[0] * bufb.shape[1]
    r_io = lax.broadcasted_iota(jnp.int32, (rows, rows), 0)
    c_io = lax.broadcasted_iota(jnp.int32, (rows, rows), 1)
    src = ((r_io >> 2) & 7) * 32 + (r_io >> 5) * 4 + (r_io & 3)
    perm = jnp.where(src == c_io, 1.0, 0.0).astype(jnp.bfloat16)
    for rel in (1, -1):
        ring[rel].wait_recv()
    to_sibling(1, -1)
    for cp in xd:
        cp.wait_recv()
    moved = jnp.dot(perm, bufb[...].reshape(rows, feat), preferred_element_type=jnp.float32)
    xp[...] = moved.astype(jnp.bfloat16).reshape(xp.shape)
    xz = []
    for s in FAR_FIRST:
        zt = (z + s) % nz
        xz.append(go(remote(xp.at[zt], bufx.at[z], xz_s.at[s - 1], xz_r.at[s - 1], (i, vz(s)))))
    bufx[z] = xp[z]

    quarter = half // 2
    for rel in (2, -2):
        ring[rel].wait_recv()
    ring[-3] = go(ring_copy(-2, 1, 4))
    ring[3] = go(ring_copy(2, -1, 5))
    fours = [go(ring_copy(-2, 2, 6, 0, quarter)), go(ring_copy(2, -2, 7, quarter, quarter))]
    to_sibling(2, -2)

    positions = prows.shape[0] // xin.shape[0]
    upad = pred.shape[0]
    loads[4].wait()
    p_r = lax.broadcasted_iota(jnp.int32, (upad, prows.shape[0]), 0)
    p_c = lax.broadcasted_iota(jnp.int32, (upad, prows.shape[0]), 1)
    pick = jnp.where(p_c == p_r * xin.shape[0] + z, 1.0, 0.0).astype(jnp.bfloat16)
    prow = jnp.dot(pick, prows[...], preferred_element_type=jnp.float32).astype(jnp.bfloat16)

    for s in range(1, nx):
        we_c[s - 1].wait_recv()
        o = 2 * ((x - s + nx) % nx) + c
        we_sib.append(
            go(remote(we.at[o], we.at[o], we_s.at[nx - 1 + s], we_r.at[nx - 1 + s], (sib, v)))
        )
    for cp in xz:
        cp.wait_recv()
    for cp in we_sib:
        cp.wait_recv()
    part[y] = tree(
        jnp.add, [jnp.dot(bufx[k], we[k], preferred_element_type=jnp.float32) for k in range(nz)]
    ).astype(jnp.bfloat16)
    ys = []
    for s in (2, 1, 3):
        ys.append(go(remote(part.at[y], part.at[y], y_s.at[s - 1], y_r.at[s - 1], (i, vy(s)))))
    for rel in (3, -3):
        ring[rel].wait_recv()
    to_sibling(3, -3)
    for s in range(1, nx):
        wp_c[s - 1].wait_recv()
        o = 2 * ((x - s + nx) % nx) + c
        wp_sib.append(
            go(remote(wp.at[o], wp.at[o], wp_s.at[nx - 1 + s], wp_r.at[nx - 1 + s], (sib, v)))
        )
    for cp in wp_sib:
        cp.wait_recv()
    pp = jnp.dot(prow, wp[...].reshape(-1, width), preferred_element_type=jnp.float32)
    pred[...] = pp.astype(jnp.bfloat16).astype(jnp.float32)
    for rel in RELS[1:5]:
        sibs[rel].wait_recv()

    n_lab = labels.shape[1]
    loads[5].wait()
    lab_rows = jnp.broadcast_to(labels[pl.ds(z, 1), :], (n_lab, n_lab)).astype(jnp.float32).T
    lab_rows = jnp.concatenate([lab_rows, jnp.zeros((16, n_lab), jnp.float32)], axis=0)
    lane = lax.broadcasted_iota(jnp.int32, lab_rows.shape, 1)

    def label_hot(p):
        zo = (z + RELS[p] + nz) % nz
        gid = (lane + (zo * NY + y) * block_cols).astype(jnp.float32)
        return jnp.where(lab_rows == gid, 1.0, 0.0).astype(jnp.bfloat16)

    def label_part(p):
        return jnp.dot(
            label_hot(p),
            wt[p * block_cols : (p + 1) * block_cols, :],
            preferred_element_type=jnp.float32,
        )

    cells = 8 * frames
    n_blocks = wlab.shape[0]
    nvoc = nz * block_cols
    near = 5
    lab_near = tree(jnp.add, [label_part(p) for p in range(near)])
    lab_near_s[...] = lab_near
    far_hot[...] = jnp.concatenate([label_hot(p) for p in range(near, nz)], axis=1)
    near_rows = near * block_cols
    far_rows = nvoc - near_rows
    for cp in fours:
        cp.wait_recv()
    to_sibling(4)
    for cp in ys:
        cp.wait_recv()
    enc[...] = tree(jnp.add, [part[k].astype(jnp.float32) for k in range(NY)]).astype(jnp.bfloat16).astype(jnp.float32)

    def make_hidden(kk, dst, n=8):
        ev = enc[...]
        for s in range(n):
            h = jnp.tanh(ev + pred[pl.ds(kk * 8 + s, 1), :])
            dst[s * frames : (s + 1) * frames, :] = h.astype(jnp.bfloat16)

    def multiply_near(src, dst, n=None):
        n = n or cells
        hv = src[0:n, :]
        first = 2 * block_cols
        for lo, hi in ((0, near_rows),):
            dst[lo:hi, 0:n] = lax.dot_general(
                wt[lo:hi, :], hv, NT, preferred_element_type=jnp.float32
            )

    def multiply_far(kk, src, last, dst, n=None):
        n = n or cells
        last[far_rows:, :] = wlab[kk]
        dst[near_rows:, 0:n] = lax.dot_general(
            last[...], src[0:n, :], NT, preferred_element_type=jnp.float32
        )

    def multiply(kk, src, last, dst, n=None):
        multiply_near(src, dst, n)
        multiply_far(kk, src, last, dst, n)

    for k in range(PRE):
        make_hidden(k, hid_pre.at[k])
        multiply_near(hid_pre.at[k], lg_pre.at[k])
    make_hidden(PRE, hid_a)
    for rel in RELS[near:]:
        sibs[rel].wait_recv()
    lab_far = jnp.dot(
        far_hot[...], wt[near * block_cols :, :], preferred_element_type=jnp.float32
    )
    lab_acc = lab_near_s[...] + lab_far
    blank_rows = lab_acc[n_lab + 8 : n_lab + 16, :]
    for k in range(n_blocks):
        both = jnp.concatenate([lab_acc[8 * k : 8 * k + 8, :], blank_rows], axis=0)
        wlab[k] = both.astype(jnp.bfloat16)
    last_a[0:far_rows, :] = wt[near_rows:, :]
    last_b[0:far_rows, :] = wt[near_rows:, :]

    sub_r = lax.broadcasted_iota(jnp.int32, (16, cells), 0)
    sub_l = lax.broadcasted_iota(jnp.int32, (16, cells), 1) // frames
    label_mask = sub_r == sub_l

    def reduce_block(src, n=None):
        n = n or cells
        m = jnp.max(src[0:nvoc, 0:n], axis=0, keepdims=True)
        t = jnp.sum(jnp.exp(src[0:nvoc, 0:n] - m), axis=0, keepdims=True)
        ll = src[nvoc : nvoc + 16, 0:n]
        label = jnp.sum(jnp.where(label_mask[:, 0:n], ll, 0.0), axis=0, keepdims=True)
        return m + jnp.log(t), label, ll[8:9, :]

    def keep(g, k, src):
        for a, val in enumerate(reduce_block(src)):
            stat[y, g, a, pl.ds(k, 1), :] = val

    sts = []

    def send_stats(ref, g):
        for s in (2, 1, 3):
            idx = g * (NY - 1) + s - 1
            sts.append(go(remote(ref, ref, st_s.at[idx], st_r.at[idx], (i, vy(s)))))

    for k in range(PRE):
        multiply_far(k, hid_pre.at[k], last_b if k % 2 else last_a, lg_pre.at[k])
        if k:
            keep(0, k - 1, lg_pre.at[k - 1])
    make_hidden(PRE + 1, hid_b)
    multiply(PRE, hid_a, last_a, lg_a)
    keep(0, PRE - 1, lg_pre.at[PRE - 1])

    def two_blocks(j, unused, g):
        k = 2 * j
        make_hidden(k + 2, hid_a)
        multiply(k + 1, hid_b, last_b, lg_b)
        keep(g, k - 8 * g, lg_a)
        make_hidden(k + 3, hid_b)
        multiply(k + 2, hid_a, last_a, lg_a)
        keep(g, k + 1 - 8 * g, lg_b)
        return unused

    lax.fori_loop(PRE // 2, 4, functools.partial(two_blocks, g=0), 0)
    send_stats(stat.at[y, 0], 0)
    lax.fori_loop(4, 7, functools.partial(two_blocks, g=1), 0, unroll=3)
    lead = 128
    make_hidden(n_blocks - 1, hid_a, lead // frames)
    multiply(n_blocks - 2, hid_b, last_b, lg_b)
    keep(1, n_blocks - 3 - 8, lg_a)
    send_stats(stat.at[y, 1], 1)
    multiply(n_blocks - 1, hid_a, last_a, lg_a, lead)
    for a, val in enumerate(reduce_block(lg_b)):
        stat2[y, 2 * a : 2 * a + 1, :] = val
    for a, val in enumerate(reduce_block(lg_a, lead)):
        stat2[y, 2 * a + 1 : 2 * a + 2, 0:lead] = val
    send_stats(stat2.at[y], 2)
    loads[6].wait()
    loads[7].wait()
    t_len = flen[z]
    u_len = llen[z]

    for cp in sts:
        cp.wait_recv()
    row8 = lax.broadcasted_iota(jnp.int32, stat.shape[3:], 0)

    def rows_of(k, g, a):
        if g == 0:
            return stat[k, 0, a]
        if g == 1:
            return jnp.where(row8 == 7, stat2[k, 2 * a : 2 * a + 1, :], stat[k, 1, a])
        return jnp.where(row8 == 0, stat2[k, 2 * a + 1 : 2 * a + 2, :], 0.0)

    for g in range(3):
        log_norm = lse([rows_of(k, g, 0) for k in range(NY)])
        label_lp = tree(jnp.add, [rows_of(k, g, 1) for k in range(NY)]) - log_norm
        blank_lp = rows_of(0, g, 2) - log_norm
        for a, val in enumerate((label_lp, blank_lp)):
            for s in range(8):
                h = val[:, 128 * (s // 4) : 128 * (s // 4) + 128]
                if s % 4:
                    h = pltpu.roll(h, 128 - 32 * (s % 4), 1)
                lp[a, pl.ds(64 * g + s, 8, stride=8), :] = h

    n = lp.shape[1] - SPARE
    lanes = lax.broadcasted_iota(jnp.int32, (n, 128), 1)
    upos = lax.broadcasted_iota(jnp.int32, (n, 128), 0)
    label_lp = lp[0, 0:n, :]
    blank_lp = lp[1, 0:n, :]
    last = jnp.where((lanes == t_len - 1) & (upos == u_len), blank_lp, 0.0)
    last = jnp.sum(jnp.sum(last, axis=0, keepdims=True), axis=1, keepdims=True)
    label_lp = jnp.where((lanes == t_len - 1) & (upos >= u_len), 0.0, label_lp)
    blank_lp = jnp.where((lanes == t_len - 2) & (upos > u_len), NEG, blank_lp)
    for bit in range(5):
        moves = (lanes >> bit) & 1 == 1
        label_lp = jnp.where(moves, pltpu.roll(label_lp, 1 << bit, 0), label_lp)
        blank_lp = jnp.where(moves, pltpu.roll(blank_lp, 1 << bit, 0), blank_lp)
    lp[0, 0:n, :] = label_lp
    lp[1, 0:n, :] = jnp.where(lanes == 0, NEG, pltpu.roll(blank_lp, 1, 1))

    for src_ref, dst_ref in ((lp, band2), (band2, band4), (band4, band8)):
        n = n // 2
        lo = [src_ref[k, pl.ds(0, n, stride=2), :] for k in range(src_ref.shape[0])]
        hi = [src_ref[k, pl.ds(1, n, stride=2), :] for k in range(src_ref.shape[0])]
        for k, val in enumerate(compose(lo, hi)):
            dst_ref[k, 0:n, :] = val

    lane8 = lax.broadcasted_iota(jnp.int32, (8, 128), 1)
    state0[0] = jnp.where(lane8 == 0, 0.0, NEG)
    state0[1] = jnp.ones((8, 128), jnp.float32)

    def advance(d, state):
        e, m = state
        nb = band8.shape[0]
        terms = [
            (pltpu.roll(e, j, 1) if j else e)
            + jnp.broadcast_to(band8[j, pl.ds(d, 1), :], (8, 128))
            for j in range(nb)
        ]
        top = tree(jnp.maximum, terms)
        m2 = tree(
            jnp.add,
            [(pltpu.roll(m, j, 1) if j else m) * jnp.exp(terms[j] - top) for j in range(nb)],
        )
        return top, m2

    e, m = lax.fori_loop(0, 20, advance, (state0[0], state0[1]), unroll=4)
    val = jnp.where(lane8 == t_len - 1, e + jnp.log(m), 0.0)
    val = jnp.sum(val, axis=1, keepdims=True) + last
    loss = -val / (t_len + u_len).astype(jnp.float32)
    lossbuf[z] = jnp.broadcast_to(loss, (8, 128))
    los = []
    for s in FAR_FIRST:
        los.append(
            go(remote(lossbuf.at[z], lossbuf.at[z], lo_s.at[s - 1], lo_r.at[s - 1], (i, vz(s))))
        )
    for cp in sends[: -len(los)]:
        cp.wait_send()
    for cp in los:
        cp.wait_recv()
    for k in range(nz):
        out[k : k + 1, :] = lossbuf[k, 0:1, :]
    for cp in los:
        cp.wait_send()


def shards(ndp, nv, encoder_rows, predictor_rows, enc_weight, pred_weight, out_weight, flen, llen, labels):
    utts, fr, feat = encoder_rows.shape
    nz = nv // NY
    per, positions, pwidth = predictor_rows.shape
    width = enc_weight.shape[1]
    frames = fr * ndp
    cols = out_weight.shape[1]
    n_blocks = (positions + 7) // 8
    groups = (n_blocks + 7) // 8
    cells = 8 * frames
    xt = jnp.transpose(encoder_rows, (1, 2, 0)).reshape(fr * feat, utts)
    prows = jnp.transpose(predictor_rows, (1, 0, 2)).reshape(positions * per, pwidth)
    vm = pl.BlockSpec(memory_space=pltpu.VMEM)
    hbm = pl.BlockSpec(memory_space=pltpu.HBM)
    dma = pltpu.SemaphoreType.DMA
    bf, f32, i32 = jnp.bfloat16, jnp.float32, jnp.int32
    nx = ndp // 2

    def pair(n):
        return [dma((n,)), dma((n,))]

    res = pl.pallas_call(
        functools.partial(joint_kernel, ndp, nv),
        out_shape=jax.ShapeDtypeStruct((per, 128), f32),
        in_specs=[hbm] * 8,
        out_specs=vm,
        scratch_shapes=[
            pltpu.VMEM(xt.shape, bf),
            pltpu.VMEM(prows.shape, bf),
            pltpu.VMEM(out_weight.shape, bf),
            pltpu.VMEM((2 * labels.shape[0], labels.shape[1]), i32),
            pltpu.SMEM(flen.shape, i32),
            pltpu.SMEM(llen.shape, i32),
            pltpu.VMEM((ndp, per * fr, feat), bf),
            pltpu.VMEM((ndp, per * fr, feat), bf),
            pltpu.VMEM((nz, frames, feat), bf),
            pltpu.VMEM((nz, frames, feat), bf),
            pltpu.VMEM((ndp, feat, width), bf),
            pltpu.VMEM((ndp, pred_weight.shape[0], width), bf),
            pltpu.VMEM((NY, frames, width), bf),
            pltpu.VMEM((frames, width), f32),
            pltpu.VMEM((8 * n_blocks + 8, width), f32),
            pltpu.VMEM((nz * cols, width), bf),
            pltpu.VMEM((n_blocks, 16, width), bf),
            pltpu.VMEM((cells, width), bf),
            pltpu.VMEM((cells, width), bf),
            pltpu.VMEM((3 * cols + 16, width), bf),
            pltpu.VMEM((3 * cols + 16, width), bf),
            pltpu.VMEM((labels.shape[1] + 16, width), f32),
            pltpu.VMEM((labels.shape[1] + 16, (nz - 5) * cols), bf),
            pltpu.VMEM((PRE, cells, width), bf),
            pltpu.VMEM((PRE, nz * cols + 16, cells), f32),
            pltpu.VMEM((nz * cols + 16, cells), f32),
            pltpu.VMEM((nz * cols + 16, cells), f32),
            pltpu.VMEM((NY + 1, groups - 1, 3, 8, cells), f32),
            pltpu.VMEM((NY, 8, cells), f32),
            pltpu.VMEM((2, 64 * groups + SPARE, 128), f32),
            pltpu.VMEM((3, 32 * groups + SPARE, 128), f32),
            pltpu.VMEM((5, 16 * groups + SPARE, 128), f32),
            pltpu.VMEM((9, 8 * groups + SPARE, 128), f32),
            pltpu.VMEM((nz, 8, 128), f32),
            pltpu.VMEM((2, 8, 128), f32),
            dma((8,)),
            *pair(ndp - 1),
            *pair(nz - 1),
            *pair(2 * nx - 1),
            *pair(2 * nx - 1),
            *pair(nz),
            *pair(nz - 1),
            *pair(NY - 1),
            *pair(groups * (NY - 1)),
            *pair(nz - 1),
        ],
        compiler_params=pltpu.CompilerParams(
            collective_id=0, has_side_effects=True, vmem_limit_bytes=60 * 1024 * 1024
        ),
    )(xt, prows, enc_weight, pred_weight, out_weight, flen, llen, labels)
    return res[:, 0]


def solution(mesh):
    return jax.shard_map(
        functools.partial(shards, mesh.shape["dp"], mesh.shape["vocab"]),
        mesh=mesh,
        in_specs=(
            P(None, "dp", "vocab"),
            P("dp", None, None),
            P("dp", None),
            P("dp", None),
            P(None, "vocab"),
            P("dp"),
            P("dp"),
            P("dp", None),
        ),
        out_specs=P("dp"),
        check_vma=False,
    )
```

```python
import functools

import jax
import jax.numpy as jnp
from jax import lax
from jax.experimental import pallas as pl
from jax.experimental.pallas import tpu as pltpu
from jax.sharding import PartitionSpec as P

MESH = pl.DeviceIdType.MESH
NY = 4
NEG = -1e30
FAR_FIRST = (4, 3, 5, 2, 6, 1, 7)
PRE = 8
SPARE = 16
NT = (((1,), (1,)), ((), ()))


RELS = (0, 1, -1, 2, -2, 3, -3, 4)


def lse(terms):
    if len(terms) == 1:
        return terms[0]
    top = functools.reduce(jnp.maximum, terms)
    return top + jnp.log(tree(jnp.add, [jnp.exp(a - top) for a in terms]))


def tree(op, vals):
    vals = list(vals)
    while len(vals) > 1:
        vals = [op(vals[k], vals[k + 1]) if k + 1 < len(vals) else vals[k] for k in range(0, len(vals), 2)]
    return vals[0]


def compose(lo, hi):
    n = len(lo)
    moved = [[pltpu.roll(b, a, 1) if a else b for b in lo] for a in range(n)]
    return [
        lse([hi[a] + moved[a][j - a] for a in range(n) if 0 <= j - a < n]) for j in range(2 * n - 1)
    ]


def joint_kernel(
    ndp,
    nv,
    xt_h,
    prows_h,
    wenc_h,
    wpred_h,
    wout_h,
    flen_h,
    llen_h,
    labels_h,
    out,
    xt,
    prows,
    wout,
    labels,
    flen,
    llen,
    xin,
    bufb,
    xp,
    bufx,
    we,
    wp,
    part,
    enc,
    pred,
    wt,
    wlab,
    hid_a,
    hid_b,
    last_a,
    last_b,
    lab_near_s,
    far_hot,
    hid_pre,
    lg_pre,
    lg_a,
    lg_b,
    stat,
    stat2,
    lp,
    band2,
    band4,
    band8,
    lossbuf,
    state0,
    in_s,
    xd_s,
    xd_r,
    xz_s,
    xz_r,
    we_s,
    we_r,
    wp_s,
    wp_r,
    ring_s,
    ring_r,
    sib_s,
    sib_r,
    y_s,
    y_r,
    st_s,
    st_r,
    lo_s,
    lo_r,
):
    nz = nv // NY
    nx = ndp // 2
    i = lax.axis_index("dp")
    v = lax.axis_index("vocab")
    z = v // NY
    y = v % NY
    x = i // 2
    c = i % 2
    sib = 2 * x + (1 - c)
    frames = part.shape[1]
    width = part.shape[2]
    feat = we.shape[1]

    def vz(s):
        return ((z + s + nz) % nz) * NY + y

    def vy(s):
        return z * NY + (y + s) % NY

    barrier = pltpu.get_barrier_semaphore()
    for s in FAR_FIRST:
        pl.semaphore_signal(barrier, inc=1, device_id=(i, vz(s)), device_id_type=MESH)
    for s in range(1, ndp):
        pl.semaphore_signal(barrier, inc=1, device_id=((i + s) % ndp, v), device_id_type=MESH)
    for s in range(1, NY):
        pl.semaphore_signal(barrier, inc=1, device_id=(i, vy(s)), device_id_type=MESH)

    erow = pl.multiple_of(feat * y, 16)
    loads = []
    for k, (src, dst) in enumerate(
        (
            (xt_h, xt),
            (wout_h, wout),
            (wenc_h.at[pl.ds(erow, feat)], we.at[i]),
            (wpred_h, wp.at[i]),
            (prows_h, prows),
            (labels_h, labels.at[pl.ds(0, labels_h.shape[0])]),
            (flen_h, flen),
            (llen_h, llen),
        )
    ):
        cp = pltpu.make_async_copy(src, dst, in_s.at[k])
        cp.start()
        loads.append(cp)

    def remote(src, dst, ssem, rsem, dev):
        return pltpu.make_async_remote_copy(
            src_ref=src, dst_ref=dst, send_sem=ssem, recv_sem=rsem, device_id=dev, device_id_type=MESH
        )

    sends = []

    def go(cp):
        cp.start()
        sends.append(cp)
        return cp

    utts = xt.shape[1]
    fr = xt.shape[0] // feat
    mine = utts * fr
    r_io = lax.broadcasted_iota(jnp.int32, (mine, utts), 0)
    u_io = lax.broadcasted_iota(jnp.int32, (mine, utts), 1)
    loads[0].wait()
    moved = None
    for f in range(fr):
        pick = jnp.where(r_io == u_io * fr + f, 1.0, 0.0).astype(jnp.bfloat16)
        one = lax.dot_general(
            pick, xt[f * feat : (f + 1) * feat, :], NT, preferred_element_type=jnp.float32
        )
        moved = one if moved is None else moved + one
    xin[...] = moved.astype(jnp.bfloat16).reshape(xin.shape)
    bufb[i] = xin[i]
    block_cols = wout.shape[1]
    loads[1].wait()
    wt[0:block_cols, :] = wout[...].astype(jnp.float32).T.astype(jnp.bfloat16)
    stat[y, 1] = jnp.zeros(stat.shape[2:], jnp.float32)
    stat2[y] = jnp.zeros(stat2.shape[1:], jnp.float32)
    loads[2].wait()
    loads[3].wait()

    pl.semaphore_wait(barrier, (ndp - 1) + (nz - 1) + (NY - 1))

    xd = []
    for s in (4, 3, 5, 2, 6, 1, 7):
        k = (i + s) % ndp
        xd.append(go(remote(xin.at[k], bufb.at[i], xd_s.at[s - 1], xd_r.at[s - 1], (k, v))))

    half = block_cols // 2

    def slot(rel, lo=0, n=half):
        start = RELS.index(rel) * block_cols + c * half + lo
        return wt.at[pl.ds(pl.multiple_of(start, 16), n)]

    def ring_copy(rel, hop, idx, lo=0, n=half):
        to = rel - hop
        to = nz // 2 if abs(to) == nz // 2 else to
        return remote(
            slot(rel, lo, n), slot(to, lo, n), ring_s.at[idx], ring_r.at[idx], (i, vz(hop))
        )

    def sib_copy(rel):
        idx = RELS.index(rel) - 1
        return remote(slot(rel), slot(rel), sib_s.at[idx], sib_r.at[idx], (sib, v))

    ring = {}
    for idx, hop in enumerate((1, -1, 2, -2)):
        ring[-hop] = go(ring_copy(0, hop, idx))
    sibs = {}

    we_c, wp_c = [], []
    for s in range(1, nx):
        dev = (2 * ((x + s) % nx) + c, v)
        we_c.append(go(remote(we.at[i], we.at[i], we_s.at[s - 1], we_r.at[s - 1], dev)))
    we_sib = [go(remote(we.at[i], we.at[i], we_s.at[nx - 1], we_r.at[nx - 1], (sib, v)))]
    for s in range(1, nx):
        dev = (2 * ((x + s) % nx) + c, v)
        wp_c.append(go(remote(wp.at[i], wp.at[i], wp_s.at[s - 1], wp_r.at[s - 1], dev)))
    wp_sib = [go(remote(wp.at[i], wp.at[i], wp_s.at[nx - 1], wp_r.at[nx - 1], (sib, v)))]

    def to_sibling(*rels):
        for rel in rels:
            sibs[rel] = go(sib_copy(rel))

    rows = bufb.shape[0] * bufb.shape[1]
    r_io = lax.broadcasted_iota(jnp.int32, (rows, rows), 0)
    c_io = lax.broadcasted_iota(jnp.int32, (rows, rows), 1)
    src = ((r_io >> 2) & 7) * 32 + (r_io >> 5) * 4 + (r_io & 3)
    perm = jnp.where(src == c_io, 1.0, 0.0).astype(jnp.bfloat16)
    for cp in xd:
        cp.wait_recv()
    moved = jnp.dot(perm, bufb[...].reshape(rows, feat), preferred_element_type=jnp.float32)
    xp[...] = moved.astype(jnp.bfloat16).reshape(xp.shape)
    xz = []
    for s in FAR_FIRST:
        zt = (z + s) % nz
        xz.append(go(remote(xp.at[zt], bufx.at[z], xz_s.at[s - 1], xz_r.at[s - 1], (i, vz(s)))))
    bufx[z] = xp[z]
    for rel in (1, -1):
        ring[rel].wait_recv()
    to_sibling(1, -1)

    quarter = half // 2
    for rel in (2, -2):
        ring[rel].wait_recv()
    ring[-3] = go(ring_copy(-2, 1, 4))
    ring[3] = go(ring_copy(2, -1, 5))
    fours = [go(ring_copy(-2, 2, 6, 0, quarter)), go(ring_copy(2, -2, 7, quarter, quarter))]
    to_sibling(2, -2)

    positions = prows.shape[0] // xin.shape[0]
    upad = pred.shape[0]
    loads[4].wait()
    p_r = lax.broadcasted_iota(jnp.int32, (upad, prows.shape[0]), 0)
    p_c = lax.broadcasted_iota(jnp.int32, (upad, prows.shape[0]), 1)
    pick = jnp.where(p_c == p_r * xin.shape[0] + z, 1.0, 0.0).astype(jnp.bfloat16)
    prow = jnp.dot(pick, prows[...], preferred_element_type=jnp.float32).astype(jnp.bfloat16)

    for s in range(1, nx):
        we_c[s - 1].wait_recv()
        o = 2 * ((x - s + nx) % nx) + c
        we_sib.append(
            go(remote(we.at[o], we.at[o], we_s.at[nx - 1 + s], we_r.at[nx - 1 + s], (sib, v)))
        )
    for cp in xz:
        cp.wait_recv()
    for cp in we_sib:
        cp.wait_recv()
    part[y] = tree(
        jnp.add, [jnp.dot(bufx[k], we[k], preferred_element_type=jnp.float32) for k in range(nz)]
    ).astype(jnp.bfloat16)
    ys = []
    for s in (2, 1, 3):
        ys.append(go(remote(part.at[y], part.at[y], y_s.at[s - 1], y_r.at[s - 1], (i, vy(s)))))
    for rel in (3, -3):
        ring[rel].wait_recv()
    to_sibling(3, -3)
    for s in range(1, nx):
        wp_c[s - 1].wait_recv()
        o = 2 * ((x - s + nx) % nx) + c
        wp_sib.append(
            go(remote(wp.at[o], wp.at[o], wp_s.at[nx - 1 + s], wp_r.at[nx - 1 + s], (sib, v)))
        )
    for cp in wp_sib:
        cp.wait_recv()
    pp = jnp.dot(prow, wp[...].reshape(-1, width), preferred_element_type=jnp.float32)
    pred[...] = pp.astype(jnp.bfloat16).astype(jnp.float32)
    for rel in RELS[1:5]:
        sibs[rel].wait_recv()

    n_lab = labels.shape[1]
    loads[5].wait()
    lab_rows = jnp.broadcast_to(labels[pl.ds(z, 1), :], (n_lab, n_lab)).astype(jnp.float32).T
    lab_rows = jnp.concatenate([lab_rows, jnp.zeros((16, n_lab), jnp.float32)], axis=0)
    lane = lax.broadcasted_iota(jnp.int32, lab_rows.shape, 1)

    def label_hot(p):
        zo = (z + RELS[p] + nz) % nz
        gid = (lane + (zo * NY + y) * block_cols).astype(jnp.float32)
        return jnp.where(lab_rows == gid, 1.0, 0.0).astype(jnp.bfloat16)

    def label_part(p):
        return jnp.dot(
            label_hot(p),
            wt[p * block_cols : (p + 1) * block_cols, :],
            preferred_element_type=jnp.float32,
        )

    cells = 8 * frames
    n_blocks = wlab.shape[0]
    nvoc = nz * block_cols
    near = 5
    lab_near = tree(jnp.add, [label_part(p) for p in range(near)])
    lab_near_s[...] = lab_near
    far_hot[...] = jnp.concatenate([label_hot(p) for p in range(near, nz)], axis=1)
    near_rows = near * block_cols
    far_rows = nvoc - near_rows
    for cp in fours:
        cp.wait_recv()
    to_sibling(4)
    for cp in ys:
        cp.wait_recv()
    enc[...] = tree(jnp.add, [part[k].astype(jnp.float32) for k in range(NY)]).astype(jnp.bfloat16).astype(jnp.float32)

    def make_hidden(kk, dst, n=8):
        ev = enc[...]
        for s in range(n):
            h = jnp.tanh(ev + pred[pl.ds(kk * 8 + s, 1), :])
            dst[s * frames : (s + 1) * frames, :] = h.astype(jnp.bfloat16)

    def multiply_near(src, dst, n=None):
        n = n or cells
        hv = src[0:n, :]
        first = 2 * block_cols
        for lo, hi in ((0, near_rows),):
            dst[lo:hi, 0:n] = lax.dot_general(
                wt[lo:hi, :], hv, NT, preferred_element_type=jnp.float32
            )

    def multiply_far(kk, src, last, dst, n=None):
        n = n or cells
        last[far_rows:, :] = wlab[kk]
        dst[near_rows:, 0:n] = lax.dot_general(
            last[...], src[0:n, :], NT, preferred_element_type=jnp.float32
        )

    def multiply(kk, src, last, dst, n=None):
        multiply_near(src, dst, n)
        multiply_far(kk, src, last, dst, n)

    for k in range(PRE):
        make_hidden(k, hid_pre.at[k])
        multiply_near(hid_pre.at[k], lg_pre.at[k])
    make_hidden(PRE, hid_a)
    for rel in RELS[near:]:
        sibs[rel].wait_recv()
    lab_far = jnp.dot(
        far_hot[...], wt[near * block_cols :, :], preferred_element_type=jnp.float32
    )
    lab_acc = lab_near_s[...] + lab_far
    blank_rows = lab_acc[n_lab + 8 : n_lab + 16, :]
    for k in range(n_blocks):
        both = jnp.concatenate([lab_acc[8 * k : 8 * k + 8, :], blank_rows], axis=0)
        wlab[k] = both.astype(jnp.bfloat16)
    last_a[0:far_rows, :] = wt[near_rows:, :]
    last_b[0:far_rows, :] = wt[near_rows:, :]

    sub_r = lax.broadcasted_iota(jnp.int32, (16, cells), 0)
    sub_l = lax.broadcasted_iota(jnp.int32, (16, cells), 1) // frames
    label_mask = sub_r == sub_l

    def reduce_block(src, n=None):
        n = n or cells
        m = jnp.max(src[0:nvoc, 0:n], axis=0, keepdims=True)
        t = jnp.sum(jnp.exp(src[0:nvoc, 0:n] - m), axis=0, keepdims=True)
        ll = src[nvoc : nvoc + 16, 0:n]
        label = jnp.sum(jnp.where(label_mask[:, 0:n], ll, 0.0), axis=0, keepdims=True)
        return m + jnp.log(t), label, ll[8:9, :]

    def keep(g, k, src):
        for a, val in enumerate(reduce_block(src)):
            stat[y, g, a, pl.ds(k, 1), :] = val

    sts = []

    def send_stats(ref, g):
        for s in (2, 1, 3):
            idx = g * (NY - 1) + s - 1
            sts.append(go(remote(ref, ref, st_s.at[idx], st_r.at[idx], (i, vy(s)))))

    for k in range(PRE):
        multiply_far(k, hid_pre.at[k], last_b if k % 2 else last_a, lg_pre.at[k])
        if k:
            keep(0, k - 1, lg_pre.at[k - 1])
    make_hidden(PRE + 1, hid_b)
    multiply(PRE, hid_a, last_a, lg_a)
    keep(0, PRE - 1, lg_pre.at[PRE - 1])

    def two_blocks(j, unused, g):
        k = 2 * j
        make_hidden(k + 2, hid_a)
        multiply(k + 1, hid_b, last_b, lg_b)
        keep(g, k - 8 * g, lg_a)
        make_hidden(k + 3, hid_b)
        multiply(k + 2, hid_a, last_a, lg_a)
        keep(g, k + 1 - 8 * g, lg_b)
        return unused

    lax.fori_loop(PRE // 2, 4, functools.partial(two_blocks, g=0), 0)
    send_stats(stat.at[y, 0], 0)
    lax.fori_loop(4, 7, functools.partial(two_blocks, g=1), 0, unroll=3)
    lead = 128
    make_hidden(n_blocks - 1, hid_a, lead // frames)
    multiply(n_blocks - 2, hid_b, last_b, lg_b)
    keep(1, n_blocks - 3 - 8, lg_a)
    send_stats(stat.at[y, 1], 1)
    multiply(n_blocks - 1, hid_a, last_a, lg_a, lead)
    for a, val in enumerate(reduce_block(lg_b)):
        stat2[y, 2 * a : 2 * a + 1, :] = val
    for a, val in enumerate(reduce_block(lg_a, lead)):
        stat2[y, 2 * a + 1 : 2 * a + 2, 0:lead] = val
    send_stats(stat2.at[y], 2)
    loads[6].wait()
    loads[7].wait()
    t_len = flen[z]
    u_len = llen[z]

    for cp in sts:
        cp.wait_recv()
    row8 = lax.broadcasted_iota(jnp.int32, stat.shape[3:], 0)

    def rows_of(k, g, a):
        if g == 0:
            return stat[k, 0, a]
        if g == 1:
            return jnp.where(row8 == 7, stat2[k, 2 * a : 2 * a + 1, :], stat[k, 1, a])
        return jnp.where(row8 == 0, stat2[k, 2 * a + 1 : 2 * a + 2, :], 0.0)

    for g in range(3):
        log_norm = lse([rows_of(k, g, 0) for k in range(NY)])
        label_lp = tree(jnp.add, [rows_of(k, g, 1) for k in range(NY)]) - log_norm
        blank_lp = rows_of(0, g, 2) - log_norm
        for a, val in enumerate((label_lp, blank_lp)):
            for s in range(8):
                h = val[:, 128 * (s // 4) : 128 * (s // 4) + 128]
                if s % 4:
                    h = pltpu.roll(h, 128 - 32 * (s % 4), 1)
                lp[a, pl.ds(64 * g + s, 8, stride=8), :] = h

    n = lp.shape[1] - SPARE
    lanes = lax.broadcasted_iota(jnp.int32, (n, 128), 1)
    upos = lax.broadcasted_iota(jnp.int32, (n, 128), 0)
    label_lp = lp[0, 0:n, :]
    blank_lp = lp[1, 0:n, :]
    last = jnp.where((lanes == t_len - 1) & (upos == u_len), blank_lp, 0.0)
    last = jnp.sum(jnp.sum(last, axis=0, keepdims=True), axis=1, keepdims=True)
    label_lp = jnp.where((lanes == t_len - 1) & (upos >= u_len), 0.0, label_lp)
    blank_lp = jnp.where((lanes == t_len - 2) & (upos > u_len), NEG, blank_lp)
    for bit in range(5):
        moves = (lanes >> bit) & 1 == 1
        label_lp = jnp.where(moves, pltpu.roll(label_lp, 1 << bit, 0), label_lp)
        blank_lp = jnp.where(moves, pltpu.roll(blank_lp, 1 << bit, 0), blank_lp)
    lp[0, 0:n, :] = label_lp
    lp[1, 0:n, :] = jnp.where(lanes == 0, NEG, pltpu.roll(blank_lp, 1, 1))

    for src_ref, dst_ref in ((lp, band2), (band2, band4), (band4, band8)):
        n = n // 2
        lo = [src_ref[k, pl.ds(0, n, stride=2), :] for k in range(src_ref.shape[0])]
        hi = [src_ref[k, pl.ds(1, n, stride=2), :] for k in range(src_ref.shape[0])]
        for k, val in enumerate(compose(lo, hi)):
            dst_ref[k, 0:n, :] = val

    lane8 = lax.broadcasted_iota(jnp.int32, (8, 128), 1)
    state0[0] = jnp.where(lane8 == 0, 0.0, NEG)
    state0[1] = jnp.ones((8, 128), jnp.float32)

    def advance(d, state):
        e, m = state
        nb = band8.shape[0]
        terms = [
            (pltpu.roll(e, j, 1) if j else e)
            + jnp.broadcast_to(band8[j, pl.ds(d, 1), :], (8, 128))
            for j in range(nb)
        ]
        top = tree(jnp.maximum, terms)
        m2 = tree(
            jnp.add,
            [(pltpu.roll(m, j, 1) if j else m) * jnp.exp(terms[j] - top) for j in range(nb)],
        )
        return top, m2

    e, m = lax.fori_loop(0, 20, advance, (state0[0], state0[1]), unroll=4)
    val = jnp.where(lane8 == t_len - 1, e + jnp.log(m), 0.0)
    val = jnp.sum(val, axis=1, keepdims=True) + last
    loss = -val / (t_len + u_len).astype(jnp.float32)
    lossbuf[z] = jnp.broadcast_to(loss, (8, 128))
    los = []
    for s in FAR_FIRST:
        los.append(
            go(remote(lossbuf.at[z], lossbuf.at[z], lo_s.at[s - 1], lo_r.at[s - 1], (i, vz(s))))
        )
    for cp in sends[: -len(los)]:
        cp.wait_send()
    for cp in los:
        cp.wait_recv()
    for k in range(nz):
        out[k : k + 1, :] = lossbuf[k, 0:1, :]
    for cp in los:
        cp.wait_send()


def shards(ndp, nv, encoder_rows, predictor_rows, enc_weight, pred_weight, out_weight, flen, llen, labels):
    utts, fr, feat = encoder_rows.shape
    nz = nv // NY
    per, positions, pwidth = predictor_rows.shape
    width = enc_weight.shape[1]
    frames = fr * ndp
    cols = out_weight.shape[1]
    n_blocks = (positions + 7) // 8
    groups = (n_blocks + 7) // 8
    cells = 8 * frames
    xt = jnp.transpose(encoder_rows, (1, 2, 0)).reshape(fr * feat, utts)
    prows = jnp.transpose(predictor_rows, (1, 0, 2)).reshape(positions * per, pwidth)
    vm = pl.BlockSpec(memory_space=pltpu.VMEM)
    hbm = pl.BlockSpec(memory_space=pltpu.HBM)
    dma = pltpu.SemaphoreType.DMA
    bf, f32, i32 = jnp.bfloat16, jnp.float32, jnp.int32
    nx = ndp // 2

    def pair(n):
        return [dma((n,)), dma((n,))]

    res = pl.pallas_call(
        functools.partial(joint_kernel, ndp, nv),
        out_shape=jax.ShapeDtypeStruct((per, 128), f32),
        in_specs=[hbm] * 8,
        out_specs=vm,
        scratch_shapes=[
            pltpu.VMEM(xt.shape, bf),
            pltpu.VMEM(prows.shape, bf),
            pltpu.VMEM(out_weight.shape, bf),
            pltpu.VMEM((2 * labels.shape[0], labels.shape[1]), i32),
            pltpu.SMEM(flen.shape, i32),
            pltpu.SMEM(llen.shape, i32),
            pltpu.VMEM((ndp, per * fr, feat), bf),
            pltpu.VMEM((ndp, per * fr, feat), bf),
            pltpu.VMEM((nz, frames, feat), bf),
            pltpu.VMEM((nz, frames, feat), bf),
            pltpu.VMEM((ndp, feat, width), bf),
            pltpu.VMEM((ndp, pred_weight.shape[0], width), bf),
            pltpu.VMEM((NY, frames, width), bf),
            pltpu.VMEM((frames, width), f32),
            pltpu.VMEM((8 * n_blocks + 8, width), f32),
            pltpu.VMEM((nz * cols, width), bf),
            pltpu.VMEM((n_blocks, 16, width), bf),
            pltpu.VMEM((cells, width), bf),
            pltpu.VMEM((cells, width), bf),
            pltpu.VMEM((3 * cols + 16, width), bf),
            pltpu.VMEM((3 * cols + 16, width), bf),
            pltpu.VMEM((labels.shape[1] + 16, width), f32),
            pltpu.VMEM((labels.shape[1] + 16, (nz - 5) * cols), bf),
            pltpu.VMEM((PRE, cells, width), bf),
            pltpu.VMEM((PRE, nz * cols + 16, cells), f32),
            pltpu.VMEM((nz * cols + 16, cells), f32),
            pltpu.VMEM((nz * cols + 16, cells), f32),
            pltpu.VMEM((NY + 1, groups - 1, 3, 8, cells), f32),
            pltpu.VMEM((NY, 8, cells), f32),
            pltpu.VMEM((2, 64 * groups + SPARE, 128), f32),
            pltpu.VMEM((3, 32 * groups + SPARE, 128), f32),
            pltpu.VMEM((5, 16 * groups + SPARE, 128), f32),
            pltpu.VMEM((9, 8 * groups + SPARE, 128), f32),
            pltpu.VMEM((nz, 8, 128), f32),
            pltpu.VMEM((2, 8, 128), f32),
            dma((8,)),
            *pair(ndp - 1),
            *pair(nz - 1),
            *pair(2 * nx - 1),
            *pair(2 * nx - 1),
            *pair(nz),
            *pair(nz - 1),
            *pair(NY - 1),
            *pair(groups * (NY - 1)),
            *pair(nz - 1),
        ],
        compiler_params=pltpu.CompilerParams(
            collective_id=0, has_side_effects=True, vmem_limit_bytes=60 * 1024 * 1024
        ),
    )(xt, prows, enc_weight, pred_weight, out_weight, flen, llen, labels)
    return res[:, 0]


def solution(mesh):
    return jax.shard_map(
        functools.partial(shards, mesh.shape["dp"], mesh.shape["vocab"]),
        mesh=mesh,
        in_specs=(
            P(None, "dp", "vocab"),
            P("dp", None, None),
            P("dp", None),
            P("dp", None),
            P(None, "vocab"),
            P("dp"),
            P("dp"),
            P("dp", None),
        ),
        out_specs=P("dp"),
        check_vma=False,
    )
```
